32 devices in a mesh: groups: 2 (over y), hid: 16 (over z, x, core), mod: 1.
Axes of the slice: x: 2, y: 2, z: 4, core: 2. Of those that a mesh axis runs over, the one named last changes fastest.
Arguments:
- tokens: bfloat16 [512, 8192], P(('groups', 'hid'), 'mod'), parts along dimension 0, may hold values from -6 to 6
- out_grad: bfloat16 [512, 8192], P(('groups', 'hid'), 'mod'), parts along dimension 0, may hold values from -6 to 6
- gate_weight: bfloat16 [8192, 28672], P('mod', 'hid'), may hold values from -0.0625 to 0.0625
- up_weight: bfloat16 [8192, 28672], P('mod', 'hid'), may hold values from -0.0625 to 0.0625
- down_weight: bfloat16 [28672, 8192], P('hid', 'mod'), may hold values from -0.03125 to 0.03125
- proj_d: bfloat16 [8192, 192], P('mod'), may hold values from -0.0625 to 0.0625
- proj_ff: bfloat16 [28672, 192], P('hid'), may hold values from -0.03125 to 0.03125
- example_ids: int32 [512], P('groups'), parts along dimension 0, may hold values from 0 to 7, never falling along the last dimension, each value on 1 to 64 neighbouring positions
- test_features: bfloat16 [512, 12288], P('groups', 'hid'), parts along dimension 0, may hold values from -0.0546875 to 0.0546875
Outputs:
- features: float32 [16, 12288], P('groups', 'hid'), parts along dimension 0
- scores: float32 [16, 256], P('groups'), parts along dimension 0
The draws below stay inside these ranges and needn't reach their ends.
There are 2 independent parts, one for each index of `groups`. The reference program is written for one: setup_inputs(seed, part) draws one part's arguments, and reference() takes and returns one part's arrays. A program takes and returns all parts, laid end to end along the dimension named above; an argument that names none is the same for every part. Nothing has to cross between parts.
Inputs may be any that keep to these rules, and one draw needn't show every extreme that they name: `example_ids`: example ids never fall along the tokens; each example holds 1 to 64 tokens.
All inputs are finite; a program needn't handle non-finite values.
Results may differ from the reference program's by a relative error of at most 0.003.
Values may be sent and summed in bfloat16 or wider, within the bound.
No kernel may reach another device: no remote copies, remote signals or barrier semaphores. Data moves between devices by JAX's collectives and lax.ppermute only.
A program may use at most 192 MiB of HBM per device.

```python
import math
import jax
import jax.numpy as jnp
import numpy as np
from jax import lax

D = 8192
FF = 28672
R = 64
EX_TOK = 32
TESTS = 256
TOKENS = 256
EX = 8
FEAT = 12288


def block_scale(key, shape, split, low, high):
    gain, own = 1.0, jax.random.fold_in(key, 6)
    for position, shards_of in split:
        steps = jnp.exp(jax.random.uniform(jax.random.fold_in(own, position), (shards_of,), jnp.float32, low / len(split), high / len(split)))
        gain = gain * jnp.repeat(steps, shape[position] // shards_of).reshape([-1 if axis == position else 1 for axis in range(len(shape))])
    return gain


def split_up(amount, total, most, skew):
    loads = [(1 << 20) // math.isqrt(grade ** skew) + 1 for grade in range(2, amount + 1)]
    spare, counts = total - most - (amount - 1), [1] * (amount - 1)
    while spare > 0:
        movable = [i for i in range(amount - 1) if counts[i] < most]
        whole, budget = sum([loads[i] for i in movable]), spare
        for i in movable:
            more = min(most - counts[i], max(1, budget * loads[i] // whole), spare)
            counts[i] = counts[i] + more
            spare = spare - more
    return np.array([most] + counts)


def uneven_parts(own_key, number_of, total, limit, slope):
    if number_of == 2:
        one = jax.random.randint(own_key, (), max(1, total - limit), min(limit, total - 1) + 1)
        return jnp.stack([one, total - one])
    tallies = jnp.asarray(split_up(number_of, total, limit, slope), jnp.int32)
    couples = (number_of - 1) // 2
    donor, receiver = tallies[1:1 + 2 * couples:2], tallies[2:2 + 2 * couples:2]
    room = jnp.minimum(donor - 1, limit - receiver)
    shifted = jax.random.randint(jax.random.fold_in(own_key, 1), (couples,), 0, 1 << 20) % (room + 1)
    tallies = tallies.at[1:1 + 2 * couples:2].set(donor - shifted).at[2:2 + 2 * couples:2].set(receiver + shifted)
    return tallies[jax.random.permutation(jax.random.fold_in(own_key, 2), number_of)]


def centred(rng, extent, scale, limit, cuts=(), kind=jnp.bfloat16):
    values = jax.random.normal(rng, extent, jnp.float32) * scale
    if len(cuts) > 0:
        values = block_scale(rng, extent, cuts, -0.22, 0.18) * values
    return jnp.clip(values, min=-limit, max=limit).astype(kind)


def setup_inputs(seed: int = 0, part: int = 0) -> dict:
    key_of = jax.random.split(jax.random.key(seed), 10)
    part_splits = jax.random.split(jax.random.fold_in(key_of[9], part), 10)
    return {
        "tokens": centred(part_splits[0], (TOKENS, D), 1.0, 6.0, ((0, 16),)),
        "out_grad": centred(part_splits[1], (TOKENS, D), 1.0, 6.0, ((0, 16),)),
        "gate_weight": centred(key_of[2], (D, FF), D ** -0.5, 0.0625, ((1, 16),)),
        "up_weight": centred(key_of[3], (D, FF), D ** -0.5, 0.0625, ((1, 16),)),
        "down_weight": centred(key_of[4], (FF, D), FF ** -0.5, 0.03125, ((0, 16),)),
        "proj_d": centred(key_of[5], (D, 3 * R), D ** -0.5, 0.0625),
        "proj_ff": centred(key_of[6], (FF, 3 * R), FF ** -0.5, 0.03125, ((0, 16),)),
        "example_ids": jnp.searchsorted(jnp.cumsum(uneven_parts(part_splits[7], EX, TOKENS, 2 * EX_TOK, 1)), jnp.arange(TOKENS), side="right").astype(jnp.int32),
        "test_features": centred(part_splits[8], (TESTS, FEAT), FEAT ** -0.5, 0.0546875, ((1, 16),)),
    }


def reference(tokens, out_grad, gate_weight, up_weight, down_weight, proj_d, proj_ff, example_ids, test_features):
    gate_act = jnp.dot(tokens, gate_weight, preferred_element_type=jnp.float32)
    up_act = jnp.dot(tokens, up_weight, preferred_element_type=jnp.float32)
    hidden_grad = lax.dot_general(out_grad, down_weight, (((1,), (1,)), ((), ())), preferred_element_type=jnp.float32)
    sigmoid_gate = jax.nn.sigmoid(gate_act)
    hidden = (gate_act * sigmoid_gate * up_act).astype(jnp.bfloat16)
    gate_grad = (hidden_grad * up_act * sigmoid_gate * (1.0 + gate_act * (1.0 - sigmoid_gate))).astype(jnp.bfloat16)
    up_grad = (hidden_grad * gate_act * sigmoid_gate).astype(jnp.bfloat16)
    input_gate = jnp.dot(tokens, proj_d[:, :R], preferred_element_type=jnp.float32)
    input_up = jnp.dot(tokens, proj_d[:, R:2 * R], preferred_element_type=jnp.float32)
    output_down = jnp.dot(out_grad, proj_d[:, 2 * R:], preferred_element_type=jnp.float32)
    output_gate = jnp.dot(gate_grad, proj_ff[:, :R], preferred_element_type=jnp.float32)
    output_up = jnp.dot(up_grad, proj_ff[:, R:2 * R], preferred_element_type=jnp.float32)
    input_down = jnp.dot(hidden, proj_ff[:, 2 * R:], preferred_element_type=jnp.float32)
    outputs = jnp.stack([output_gate, output_up, output_down], axis=2)
    inputs = jnp.stack([input_gate, input_up, input_down], axis=1)
    outer = (outputs[:, :, :, None] * inputs[:, None, :, :]).reshape(outputs.shape[0], FEAT)
    member = (example_ids[None, :] == jnp.arange(EX, dtype=jnp.int32)[:, None]).astype(jnp.float32)
    features = jnp.dot(member, outer, precision=lax.Precision.HIGHEST, preferred_element_type=jnp.float32)
    scores = jnp.dot(features, test_features.astype(jnp.float32).T, precision=lax.Precision.HIGHEST, preferred_element_type=jnp.float32)
    return features, scores
```

```python
import functools

import jax
import jax.numpy as jnp
from jax import lax
from jax.experimental import pallas as pl
from jax.experimental.pallas import tpu as pltpu
from jax.sharding import PartitionSpec as P

R = 64
EX_TOK = 32
TILE = 256
DEPTH = 2048
VMEM = 56 * 1024 * 1024
HIGH = lax.Precision.HIGHEST


def project_rows(block_rows, weights):
    return jnp.dot(block_rows, weights, preferred_element_type=jnp.float32)


def local_general(
    tokens,
    out_grad,
    gate_weight,
    up_weight,
    down_weight,
    proj_d,
    proj_ff,
    example_ids,
    test_features,
):
    width = gate_weight.shape[1]
    input_proj = proj_d[:, : 2 * R]
    output_proj = proj_d[:, 2 * R :]
    block_rows = lax.all_gather(tokens, "hid", axis=0, tiled=True)
    forward = jnp.concatenate(
        [
            project_rows(block_rows, gate_weight),
            project_rows(block_rows, up_weight),
            project_rows(block_rows, input_proj),
        ],
        axis=1,
    )
    block_rows = lax.all_gather(out_grad, "hid", axis=0, tiled=True)
    spread = lax.dot_general(
        block_rows, down_weight, (((1,), (1,)), ((), ())), preferred_element_type=jnp.float32
    )
    backward = jnp.concatenate([spread, project_rows(block_rows, output_proj)], axis=1)
    forward = lax.psum(forward, "mod")
    backward = lax.psum(backward, "mod")
    gate_act = forward[:, :width]
    up_act = forward[:, width : 2 * width]
    input_gate = forward[:, 2 * width : 2 * width + R]
    input_up = forward[:, 2 * width + R :]
    hidden_grad = backward[:, :width]
    output_down = backward[:, width:]
    hidden, gate_grad, up_grad = pointwise(gate_act, up_act, hidden_grad)
    output_gate = project_rows(gate_grad, proj_ff[:, :R])
    output_up = project_rows(up_grad, proj_ff[:, R : 2 * R])
    input_down = project_rows(hidden, proj_ff[:, 2 * R :])
    shares = R // lax.axis_size("hid")
    offset = lax.axis_index("hid") * shares
    output_gate, output_up, input_down = lax.psum((output_gate, output_up, input_down), "hid")
    own_gate = lax.dynamic_slice_in_dim(output_gate, offset, shares, 1)
    own_up = lax.dynamic_slice_in_dim(output_up, offset, shares, 1)
    own_down = lax.dynamic_slice_in_dim(output_down, offset, shares, 1)
    outputs = jnp.stack([own_gate, own_up, own_down], axis=2)
    inputs = jnp.stack([input_gate, input_up, input_down], axis=1)
    total_rows = outputs.shape[0]
    outer = (outputs[:, :, :, None] * inputs[:, None, :, :]).reshape(total_rows, shares * 3 * R)
    examples = example_ids.shape[0] // EX_TOK
    member = (example_ids[None, :] == jnp.arange(examples, dtype=jnp.int32)[:, None]).astype(
        jnp.float32
    )
    features = jnp.dot(member, outer, precision=HIGH, preferred_element_type=jnp.float32)
    partial_scores = jnp.dot(
        features,
        test_features.astype(jnp.float32).T,
        precision=HIGH,
        preferred_element_type=jnp.float32,
    )
    scores = lax.psum(partial_scores, "hid")
    return (features, scores)


def pointwise(gate_act, up_act, hidden_grad):
    sig = jax.nn.sigmoid(gate_act)
    hidden = (gate_act * sig * up_act).astype(jnp.bfloat16)
    gate_grad = (hidden_grad * up_act * sig * (1.0 + gate_act * (1.0 - sig))).astype(jnp.bfloat16)
    up_grad = (hidden_grad * gate_act * sig).astype(jnp.bfloat16)
    return hidden, gate_grad, up_grad


def ring_device(position, core, chips):
    height = chips // 2
    if isinstance(position, int):
        back = position >= height
        z = 2 * height - 1 - position if back else position
        return z * 4 + int(back) * 2 + core
    back = (position >= height).astype(jnp.int32)
    z = position + back * (2 * height - 1 - 2 * position)
    return z * 4 + back * 2 + core


def ring_position(device, chips):
    z, x = device // 4, (device // 2) % 2
    return z + x * (chips - 1 - 2 * z)


def ring_step(block, chips, step):
    pairs = [
        (ring_device(r, core, chips), ring_device((r + step) % chips, core, chips))
        for r in range(chips)
        for core in range(2)
    ]
    return lax.ppermute(block, "hid", pairs)


def core_swap(block, chips):
    return lax.ppermute(block, "hid", [(h, h ^ 1) for h in range(2 * chips)])


def gather_blocks(own, chips):
    half = own.shape[1] // 2
    found = [(0, 0, own)]
    ahead, behind = own, own
    for step in range(1, chips // 2):
        ahead = ring_step(ahead, chips, 1)
        behind = ring_step(behind, chips, -1)
        found += [(-step, 0, ahead), (step, 0, behind)]
    across = chips // 2
    found.append((across, 0, ring_step(ahead[:, :half], chips, 1)))
    found.append((across, half, ring_step(behind[:, half:], chips, -1)))
    places, blocks = [], []
    for offset, column, block in found:
        for other in range(2):
            places.append((offset, other, column))
            blocks.append(core_swap(block, chips) if other else block)
    return places, blocks


def assemble(places, chips, blocks, whole, sems):
    device = lax.axis_index("hid")
    position, core = ring_position(device, chips), device % 2
    copies = []
    for index, (offset, other, column) in enumerate(places):
        rows, columns = blocks[index].shape
        source_core = core + other - 2 * core * other
        source = ring_device((position + offset + chips) % chips, source_core, chips)
        start = pl.multiple_of(source * rows, rows)
        target = whole.at[pl.ds(start, rows), pl.ds(column, columns)]
        copies.append(pltpu.make_async_copy(blocks[index], target, sems.at[index]))
    for copy in copies:
        copy.start()
    for copy in copies:
        copy.wait()


def deep_dot(left, right, transposed, columns):
    depth = left.shape[1]
    total = jnp.zeros((left.shape[0], columns), jnp.float32)
    for start in range(0, depth, DEPTH):
        part = pl.ds(start, DEPTH)
        a = left[:, part]
        if transposed:
            total += lax.dot_general(
                a, right[:, part], (((1,), (1,)), ((), ())), preferred_element_type=jnp.float32
            )
        else:
            total += jnp.dot(a, right[part, :], preferred_element_type=jnp.float32)
    return total


def forward_kernel(places, chips, *refs):
    count = len(places)
    blocks, (weight, out, whole, sems) = refs[:count], refs[count:]

    @pl.when(pl.program_id(0) == 0)
    def _():
        assemble(places, chips, blocks, whole, sems)

    out[...] = deep_dot(whole, weight, False, out.shape[1])


def forward(places, chips, blocks, weight, tile):
    rows = blocks[0].shape[0] * chips * 2
    depth, width = weight.shape
    return pl.pallas_call(
        functools.partial(forward_kernel, places, chips),
        grid=(width // tile,),
        out_shape=jax.ShapeDtypeStruct((rows, width), jnp.float32),
        in_specs=[pl.BlockSpec(memory_space=pl.ANY)] * len(blocks)
        + [pl.BlockSpec((depth, tile), lambda n: (0, n))],
        out_specs=pl.BlockSpec((rows, tile), lambda n: (0, n)),
        scratch_shapes=[
            pltpu.VMEM((rows, depth), jnp.bfloat16),
            pltpu.SemaphoreType.DMA((len(blocks),)),
        ],
        compiler_params=pltpu.CompilerParams(vmem_limit_bytes=VMEM),
        cost_estimate=pl.CostEstimate(
            flops=2 * rows * depth * width, bytes_accessed=2 * depth * width, transcendentals=0
        ),
    )(*blocks, weight)


def membership(ids, examples):
    rows = lax.broadcasted_iota(jnp.int32, (examples, ids.shape[1]), 0)
    return (jnp.broadcast_to(ids, rows.shape) == rows).astype(jnp.float32)


def exact_dot(a, b, contract):
    return lax.dot_general(
        a, b, (contract, ((), ())), precision=HIGH, preferred_element_type=jnp.float32
    )


def backward_kernel(places, chips, examples, *refs):
    count = len(places)
    blocks = refs[:count]
    weight, gate, up, proj, proj_ff, ids, send, whole, sums, flipped, sems = refs[count:]
    step = pl.program_id(0)
    hid = 2 * chips
    shares = R // hid

    @pl.when(step == 0)
    def _():
        assemble(places, chips, blocks, whole, sems)
        sums[...] = jnp.zeros_like(sums)
        columns = deep_dot(whole, proj, False, R).T
        for lanes in range(flipped.shape[0]):
            flipped[lanes] = columns[:, lanes * 128 : (lanes + 1) * 128]

    hidden_grad = deep_dot(whole, weight, True, gate.shape[1])
    hidden, gate_grad, up_grad = pointwise(gate[...], up[...], hidden_grad)
    for m, value in enumerate((gate_grad, up_grad, hidden)):
        sums[m] += jnp.dot(
            value, proj_ff[:, m * R : (m + 1) * R], preferred_element_type=jnp.float32
        )

    @pl.when(step == pl.num_programs(0) - 1)
    def _():
        for m in range(2):
            columns = sums[m].T
            for p in range(hid):
                send[p, m * shares : (m + 1) * shares, :] = columns[p * shares : (p + 1) * shares]
        member = membership(ids[...], examples)
        total_rows = member.shape[1]
        for j in range(shares):
            every = pl.ds(j, hid, shares)
            own = jnp.concatenate([flipped[k, every, :] for k in range(flipped.shape[0])], axis=1)
            left = (own[:, None, :] * member[None, :, :]).reshape(hid * examples, total_rows)
            product = exact_dot(left, sums[2], ((1,), (0,)))
            send[:, 2 * shares :, j * R : (j + 1) * R] = product.reshape(hid, examples, R)


def backward(places, chips, blocks, weight, gate, up, proj, proj_ff, ids, tile):
    rows = blocks[0].shape[0] * chips * 2
    width, depth = weight.shape
    hid = 2 * chips
    shares, examples = R // hid, rows // EX_TOK
    return pl.pallas_call(
        functools.partial(backward_kernel, places, chips, examples),
        grid=(width // tile,),
        out_shape=jax.ShapeDtypeStruct((hid, 2 * shares + examples, rows), jnp.float32),
        in_specs=[pl.BlockSpec(memory_space=pl.ANY)] * len(blocks)
        + [
            pl.BlockSpec((tile, depth), lambda n: (n, 0)),
            pl.BlockSpec((rows, tile), lambda n: (0, n)),
            pl.BlockSpec((rows, tile), lambda n: (0, n)),
            pl.BlockSpec((depth, R), lambda n: (0, 0)),
            pl.BlockSpec((tile, 3 * R), lambda n: (n, 0)),
            pl.BlockSpec((1, rows), lambda n: (0, 0)),
        ],
        out_specs=pl.BlockSpec((hid, 2 * shares + examples, rows), lambda n: (0, 0, 0)),
        scratch_shapes=[
            pltpu.VMEM((rows, depth), jnp.bfloat16),
            pltpu.VMEM((3, rows, R), jnp.float32),
            pltpu.VMEM((rows // 128, R, 128), jnp.float32),
            pltpu.SemaphoreType.DMA((len(blocks),)),
        ],
        compiler_params=pltpu.CompilerParams(vmem_limit_bytes=VMEM),
        cost_estimate=pl.CostEstimate(
            flops=2 * rows * depth * width, bytes_accessed=2 * depth * width, transcendentals=0
        ),
    )(*blocks, weight, gate, up, proj, proj_ff, ids)


def features_kernel(hid, received, inputs, ids, tests, features, partial):
    shares = R // hid
    examples = features.shape[0]
    member = membership(ids[...], examples)
    total = jnp.sum(received[...], axis=0)
    for m in range(2):
        own = total[m * shares : (m + 1) * shares]
        left = (own[:, None, :] * member[None, :, :]).reshape(shares * examples, own.shape[1])
        product = exact_dot(left, inputs[:, m * R : (m + 1) * R], ((1,), (0,)))
        for j in range(shares):
            start = (j * 3 + m) * R
            features[:, start : start + R] = product[j * examples : (j + 1) * examples]
    for j in range(shares):
        start = (j * 3 + 2) * R
        features[:, start : start + R] = total[2 * shares :, j * R : (j + 1) * R]
    scores = exact_dot(features[...], tests[...].astype(jnp.float32), ((1,), (1,)))
    partial[...] = jnp.broadcast_to(scores[None], partial.shape)


def finish(received, inputs, ids, tests):
    hid, _, rows = received.shape
    examples = rows // EX_TOK
    vmem = pl.BlockSpec(memory_space=pltpu.VMEM)
    return pl.pallas_call(
        functools.partial(features_kernel, hid),
        out_shape=(
            jax.ShapeDtypeStruct((examples, tests.shape[1]), jnp.float32),
            jax.ShapeDtypeStruct((hid, examples, tests.shape[0]), jnp.float32),
        ),
        in_specs=[vmem] * 4,
        out_specs=(vmem, vmem),
        compiler_params=pltpu.CompilerParams(vmem_limit_bytes=VMEM),
    )(received, inputs, ids, tests)


def local_ring(
    tokens,
    out_grad,
    gate_weight,
    up_weight,
    down_weight,
    proj_d,
    proj_ff,
    example_ids,
    test_features,
):
    chips = lax.axis_size("hid") // 2
    ids = example_ids[None, :]
    places, token_blocks = gather_blocks(tokens, chips)
    _, grad_blocks = gather_blocks(out_grad, chips)
    inputs = forward(places, chips, token_blocks, proj_d[:, : 2 * R], 2 * R)
    gate = forward(places, chips, token_blocks, gate_weight, TILE)
    up = forward(places, chips, token_blocks, up_weight, TILE)
    send = backward(
        places, chips, grad_blocks, down_weight, gate, up, proj_d[:, 2 * R :], proj_ff, ids, TILE
    )
    received = lax.all_to_all(send, "hid", 0, 0)
    features, partial = finish(received, inputs, ids, test_features)
    scores = jnp.sum(lax.all_to_all(partial, "hid", 0, 0), axis=0)
    return features, scores


def solution(mesh):
    one_ring = mesh.shape["mod"] == 1 and mesh.shape["hid"] <= 16
    return jax.shard_map(
        local_ring if one_ring else local_general,
        mesh=mesh,
        in_specs=(
            P(("groups", "hid"), "mod"),
            P(("groups", "hid"), "mod"),
            P("mod", "hid"),
            P("mod", "hid"),
            P("hid", "mod"),
            P("mod", None),
            P("hid", None),
            P("groups"),
            P("groups", "hid"),
        ),
        out_specs=(P("groups", "hid"), P("groups", None)),
        check_vma=False,
    )
```

```python
import functools

import jax
import jax.numpy as jnp
from jax import lax
from jax.experimental import pallas as pl
from jax.experimental.pallas import tpu as pltpu
from jax.sharding import PartitionSpec as P

R = 64
EX_TOK = 32
TILE = 256
DEPTH = 2048
VMEM = 56 * 1024 * 1024
HIGH = lax.Precision.HIGHEST


def project_rows(block_rows, weights):
    return jnp.dot(block_rows, weights, preferred_element_type=jnp.float32)


def local_general(
    tokens,
    out_grad,
    gate_weight,
    up_weight,
    down_weight,
    proj_d,
    proj_ff,
    example_ids,
    test_features,
):
    width = gate_weight.shape[1]
    input_proj = proj_d[:, : 2 * R]
    output_proj = proj_d[:, 2 * R :]
    block_rows = lax.all_gather(tokens, "hid", axis=0, tiled=True)
    forward = jnp.concatenate(
        [
            project_rows(block_rows, gate_weight),
            project_rows(block_rows, up_weight),
            project_rows(block_rows, input_proj),
        ],
        axis=1,
    )
    block_rows = lax.all_gather(out_grad, "hid", axis=0, tiled=True)
    spread = lax.dot_general(
        block_rows, down_weight, (((1,), (1,)), ((), ())), preferred_element_type=jnp.float32
    )
    backward = jnp.concatenate([spread, project_rows(block_rows, output_proj)], axis=1)
    forward = lax.psum(forward, "mod")
    backward = lax.psum(backward, "mod")
    gate_act = forward[:, :width]
    up_act = forward[:, width : 2 * width]
    input_gate = forward[:, 2 * width : 2 * width + R]
    input_up = forward[:, 2 * width + R :]
    hidden_grad = backward[:, :width]
    output_down = backward[:, width:]
    hidden, gate_grad, up_grad = pointwise(gate_act, up_act, hidden_grad)
    output_gate = project_rows(gate_grad, proj_ff[:, :R])
    output_up = project_rows(up_grad, proj_ff[:, R : 2 * R])
    input_down = project_rows(hidden, proj_ff[:, 2 * R :])
    shares = R // lax.axis_size("hid")
    offset = lax.axis_index("hid") * shares
    output_gate, output_up, input_down = lax.psum((output_gate, output_up, input_down), "hid")
    own_gate = lax.dynamic_slice_in_dim(output_gate, offset, shares, 1)
    own_up = lax.dynamic_slice_in_dim(output_up, offset, shares, 1)
    own_down = lax.dynamic_slice_in_dim(output_down, offset, shares, 1)
    outputs = jnp.stack([own_gate, own_up, own_down], axis=2)
    inputs = jnp.stack([input_gate, input_up, input_down], axis=1)
    total_rows = outputs.shape[0]
    outer = (outputs[:, :, :, None] * inputs[:, None, :, :]).reshape(total_rows, shares * 3 * R)
    examples = example_ids.shape[0] // EX_TOK
    member = (example_ids[None, :] == jnp.arange(examples, dtype=jnp.int32)[:, None]).astype(
        jnp.float32
    )
    features = jnp.dot(member, outer, precision=HIGH, preferred_element_type=jnp.float32)
    partial_scores = jnp.dot(
        features,
        test_features.astype(jnp.float32).T,
        precision=HIGH,
        preferred_element_type=jnp.float32,
    )
    scores = lax.psum(partial_scores, "hid")
    return (features, scores)


def pointwise(gate_act, up_act, hidden_grad):
    sig = jax.nn.sigmoid(gate_act)
    hidden = (gate_act * sig * up_act).astype(jnp.bfloat16)
    gate_grad = (hidden_grad * up_act * sig * (1.0 + gate_act * (1.0 - sig))).astype(jnp.bfloat16)
    up_grad = (hidden_grad * gate_act * sig).astype(jnp.bfloat16)
    return hidden, gate_grad, up_grad


def ring_device(position, core, chips):
    height = chips // 2
    if isinstance(position, int):
        back = position >= height
        z = 2 * height - 1 - position if back else position
        return z * 4 + int(back) * 2 + core
    back = (position >= height).astype(jnp.int32)
    z = position + back * (2 * height - 1 - 2 * position)
    return z * 4 + back * 2 + core


def ring_position(device, chips):
    z, x = device // 4, (device // 2) % 2
    return z + x * (chips - 1 - 2 * z)


def ring_step(block, chips, step):
    pairs = [
        (ring_device(r, core, chips), ring_device((r + step) % chips, core, chips))
        for r in range(chips)
        for core in range(2)
    ]
    return lax.ppermute(block, "hid", pairs)


def core_swap(block, chips):
    return lax.ppermute(block, "hid", [(h, h ^ 1) for h in range(2 * chips)])


def gather_blocks(own, chips):
    half = own.shape[1] // 2
    found = [(0, 0, own)]
    ahead, behind = own, own
    for step in range(1, chips // 2):
        ahead = ring_step(ahead, chips, 1)
        behind = ring_step(behind, chips, -1)
        found += [(-step, 0, ahead), (step, 0, behind)]
    across = chips // 2
    found.append((across, 0, ring_step(ahead[:, :half], chips, 1)))
    found.append((across, half, ring_step(behind[:, half:], chips, -1)))
    places, blocks = [], []
    for offset, column, block in found:
        for other in range(2):
            places.append((offset, other, column))
            blocks.append(core_swap(block, chips) if other else block)
    return places, blocks


def assemble(places, chips, blocks, whole, sems):
    device = lax.axis_index("hid")
    position, core = ring_position(device, chips), device % 2
    copies = []
    for index, (offset, other, column) in enumerate(places):
        rows, columns = blocks[index].shape
        source_core = core + other - 2 * core * other
        source = ring_device((position + offset + chips) % chips, source_core, chips)
        start = pl.multiple_of(source * rows, rows)
        target = whole.at[pl.ds(start, rows), pl.ds(column, columns)]
        copies.append(pltpu.make_async_copy(blocks[index], target, sems.at[index]))
    for copy in copies:
        copy.start()
    for copy in copies:
        copy.wait()


def deep_dot(left, right, transposed, columns):
    depth = left.shape[1]
    total = jnp.zeros((left.shape[0], columns), jnp.float32)
    for start in range(0, depth, DEPTH):
        part = pl.ds(start, DEPTH)
        a = left[:, part]
        if transposed:
            total += last_dot(a, right[:, part])
        else:
            total += jnp.dot(a, right[part, :], preferred_element_type=jnp.float32)
    return total


def last_dot(a, b):
    return lax.dot_general(a, b, (((1,), (1,)), ((), ())), preferred_element_type=jnp.float32)


def tiled_kernel(places, chips, *refs):
    count = len(places)
    blocks, (weight, out, whole, sems) = refs[:count], refs[count:]

    @pl.when(pl.program_id(0) == 0)
    def _():
        assemble(places, chips, blocks, whole, sems)

    out[...] = deep_dot(whole, weight, False, out.shape[1])


def tiled_forward(places, chips, blocks, weight, tile):
    rows = blocks[0].shape[0] * chips * 2
    depth, width = weight.shape
    return pl.pallas_call(
        functools.partial(tiled_kernel, places, chips),
        grid=(width // tile,),
        out_shape=jax.ShapeDtypeStruct((rows, width), jnp.float32),
        in_specs=[pl.BlockSpec(memory_space=pl.ANY)] * len(blocks)
        + [pl.BlockSpec((depth, tile), lambda n: (0, n))],
        out_specs=pl.BlockSpec((rows, tile), lambda n: (0, n)),
        scratch_shapes=[
            pltpu.VMEM((rows, depth), jnp.bfloat16),
            pltpu.SemaphoreType.DMA((len(blocks),)),
        ],
        compiler_params=pltpu.CompilerParams(vmem_limit_bytes=VMEM),
        cost_estimate=pl.CostEstimate(
            flops=2 * rows * depth * width, bytes_accessed=2 * depth * width, transcendentals=0
        ),
    )(*blocks, weight)


def deep_kernel(places, chips, *refs):
    count = len(places)
    blocks, (weight, proj, out, inputs, whole, sems) = refs[:count], refs[count:]
    step = pl.program_id(0)

    @pl.when(step == 0)
    def _():
        assemble(places, chips, blocks, whole, sems)
        out[...] = jnp.zeros_like(out)
        inputs[...] = jnp.zeros_like(inputs)

    depth = weight.shape[0]
    x = whole[:, pl.ds(pl.multiple_of(step * depth, depth), depth)]
    out[...] += jnp.dot(x, weight[...], preferred_element_type=jnp.float32)
    inputs[...] += last_dot(x, proj[: 2 * R, :])


def deep_forward(places, chips, blocks, weight, proj, depth_tile):
    rows = blocks[0].shape[0] * chips * 2
    depth, width = weight.shape
    return pl.pallas_call(
        functools.partial(deep_kernel, places, chips),
        grid=(depth // depth_tile,),
        out_shape=(
            jax.ShapeDtypeStruct((rows, width), jnp.float32),
            jax.ShapeDtypeStruct((rows, 2 * R), jnp.float32),
        ),
        in_specs=[pl.BlockSpec(memory_space=pl.ANY)] * len(blocks)
        + [
            pl.BlockSpec((depth_tile, width), lambda k: (k, 0)),
            pl.BlockSpec((3 * R, depth_tile), lambda k: (0, k)),
        ],
        out_specs=(
            pl.BlockSpec((rows, width), lambda k: (0, 0)),
            pl.BlockSpec((rows, 2 * R), lambda k: (0, 0)),
        ),
        scratch_shapes=[
            pltpu.VMEM((rows, depth), jnp.bfloat16),
            pltpu.SemaphoreType.DMA((len(blocks),)),
        ],
        compiler_params=pltpu.CompilerParams(vmem_limit_bytes=VMEM),
        cost_estimate=pl.CostEstimate(
            flops=2 * rows * depth * width, bytes_accessed=2 * depth * width, transcendentals=0
        ),
    )(*blocks, weight, proj)


def membership(ids, examples):
    rows = lax.broadcasted_iota(jnp.int32, (examples, ids.shape[1]), 0)
    return (jnp.broadcast_to(ids, rows.shape) == rows).astype(jnp.float32)


def exact_dot(a, b, contract):
    return lax.dot_general(
        a, b, (contract, ((), ())), precision=HIGH, preferred_element_type=jnp.float32
    )


def backward_kernel(places, chips, examples, *refs):
    count = len(places)
    blocks = refs[:count]
    weight, gate, up, proj, proj_ff, ids, send, whole, sums, flipped, sems = refs[count:]
    step = pl.program_id(0)
    hid = 2 * chips
    shares = R // hid

    @pl.when(step == 0)
    def _():
        assemble(places, chips, blocks, whole, sems)
        sums[...] = jnp.zeros_like(sums)
        columns = jnp.zeros((R, whole.shape[0]), jnp.float32)
        for start in range(0, whole.shape[1], DEPTH):
            part = pl.ds(start, DEPTH)
            columns += last_dot(proj[2 * R :, part], whole[:, part])
        for lanes in range(flipped.shape[0]):
            flipped[lanes] = columns[:, lanes * 128 : (lanes + 1) * 128]

    hidden_grad = deep_dot(whole, weight, True, gate.shape[1])
    hidden, gate_grad, up_grad = pointwise(gate[...], up[...], hidden_grad)
    for m, value in enumerate((gate_grad, up_grad, hidden)):
        sums[m * R : (m + 1) * R, :] += last_dot(proj_ff[m * R : (m + 1) * R, :], value)

    @pl.when(step == pl.num_programs(0) - 1)
    def _():
        for m in range(2):
            for p in range(hid):
                own = sums[m * R + p * shares : m * R + (p + 1) * shares, :]
                send[p, m * shares : (m + 1) * shares, :] = own
        member = membership(ids[...], examples)
        total_rows = member.shape[1]
        for j in range(shares):
            every = pl.ds(j, hid, shares)
            own = jnp.concatenate([flipped[k, every, :] for k in range(flipped.shape[0])], axis=1)
            left = (own[:, None, :] * member[None, :, :]).reshape(hid * examples, total_rows)
            product = exact_dot(left, sums[2 * R :, :], ((1,), (1,)))
            send[:, 2 * shares :, j * R : (j + 1) * R] = product.reshape(hid, examples, R)


def backward(places, chips, blocks, weight, gate, up, proj, proj_ff, ids, tile):
    rows = blocks[0].shape[0] * chips * 2
    width, depth = weight.shape
    hid = 2 * chips
    shares, examples = R // hid, rows // EX_TOK
    return pl.pallas_call(
        functools.partial(backward_kernel, places, chips, examples),
        grid=(width // tile,),
        out_shape=jax.ShapeDtypeStruct((hid, 2 * shares + examples, rows), jnp.float32),
        in_specs=[pl.BlockSpec(memory_space=pl.ANY)] * len(blocks)
        + [
            pl.BlockSpec((tile, depth), lambda n: (n, 0)),
            pl.BlockSpec((rows, tile), lambda n: (0, n)),
            pl.BlockSpec((rows, tile), lambda n: (0, n)),
            pl.BlockSpec((3 * R, depth), lambda n: (0, 0)),
            pl.BlockSpec((3 * R, tile), lambda n: (0, n)),
            pl.BlockSpec((1, rows), lambda n: (0, 0)),
        ],
        out_specs=pl.BlockSpec((hid, 2 * shares + examples, rows), lambda n: (0, 0, 0)),
        scratch_shapes=[
            pltpu.VMEM((rows, depth), jnp.bfloat16),
            pltpu.VMEM((3 * R, rows), jnp.float32),
            pltpu.VMEM((rows // 128, R, 128), jnp.float32),
            pltpu.SemaphoreType.DMA((len(blocks),)),
        ],
        compiler_params=pltpu.CompilerParams(vmem_limit_bytes=VMEM),
        cost_estimate=pl.CostEstimate(
            flops=2 * rows * depth * width, bytes_accessed=2 * depth * width, transcendentals=0
        ),
    )(*blocks, weight, gate, up, proj, proj_ff, ids)


def features_kernel(hid, received, inputs, ids, tests, features, partial):
    shares = R // hid
    examples = features.shape[0]
    member = membership(ids[...], examples)
    total = jnp.sum(received[...], axis=0)
    for m in range(2):
        own = total[m * shares : (m + 1) * shares]
        left = (own[:, None, :] * member[None, :, :]).reshape(shares * examples, own.shape[1])
        product = exact_dot(left, inputs[:, m * R : (m + 1) * R], ((1,), (0,)))
        for j in range(shares):
            start = (j * 3 + m) * R
            features[:, start : start + R] = product[j * examples : (j + 1) * examples]
    for j in range(shares):
        start = (j * 3 + 2) * R
        features[:, start : start + R] = total[2 * shares :, j * R : (j + 1) * R]
    scores = exact_dot(features[...], tests[...].astype(jnp.float32), ((1,), (1,)))
    partial[...] = jnp.broadcast_to(scores[None], partial.shape)


def finish(received, inputs, ids, tests):
    hid, _, rows = received.shape
    examples = rows // EX_TOK
    vmem = pl.BlockSpec(memory_space=pltpu.VMEM)
    return pl.pallas_call(
        functools.partial(features_kernel, hid),
        out_shape=(
            jax.ShapeDtypeStruct((examples, tests.shape[1]), jnp.float32),
            jax.ShapeDtypeStruct((hid, examples, tests.shape[0]), jnp.float32),
        ),
        in_specs=[vmem] * 4,
        out_specs=(vmem, vmem),
        compiler_params=pltpu.CompilerParams(vmem_limit_bytes=VMEM),
    )(received, inputs, ids, tests)


def local_ring(
    tokens,
    out_grad,
    gate_weight,
    up_weight,
    down_weight,
    proj_d,
    proj_ff,
    example_ids,
    test_features,
):
    chips = lax.axis_size("hid") // 2
    ids = example_ids[None, :]
    places, token_blocks = gather_blocks(tokens, chips)
    _, grad_blocks = gather_blocks(out_grad, chips)
    gate, inputs = deep_forward(places, chips, token_blocks, gate_weight, proj_d.T, 1024)
    up = tiled_forward(places, chips, token_blocks, up_weight, up_weight.shape[1] // 2)
    send = backward(
        places, chips, grad_blocks, down_weight, gate, up, proj_d.T, proj_ff.T, ids, TILE
    )
    received = lax.all_to_all(send, "hid", 0, 0)
    features, partial = finish(received, inputs, ids, test_features)
    scores = jnp.sum(lax.all_to_all(partial, "hid", 0, 0), axis=0)
    return features, scores


def solution(mesh):
    one_ring = mesh.shape["mod"] == 1 and mesh.shape["hid"] <= 16
    return jax.shard_map(
        local_ring if one_ring else local_general,
        mesh=mesh,
        in_specs=(
            P(("groups", "hid"), "mod"),
            P(("groups", "hid"), "mod"),
            P("mod", "hid"),
            P("mod", "hid"),
            P("hid", "mod"),
            P("mod", None),
            P("hid", None),
            P("groups"),
            P("groups", "hid"),
        ),
        out_specs=(P("groups", "hid"), P("groups", None)),
        check_vma=False,
    )
```

```python
import functools

import jax
import jax.numpy as jnp
from jax import lax
from jax.experimental import pallas as pl
from jax.experimental.pallas import tpu as pltpu
from jax.sharding import PartitionSpec as P

R = 64
EX_TOK = 32
TILE = 256
DEPTH = 2048
NEAR = 4
VMEM = 56 * 1024 * 1024
HIGH = lax.Precision.HIGHEST


def project_rows(block_rows, weights):
    return jnp.dot(block_rows, weights, preferred_element_type=jnp.float32)


def local_general(
    tokens,
    out_grad,
    gate_weight,
    up_weight,
    down_weight,
    proj_d,
    proj_ff,
    example_ids,
    test_features,
):
    width = gate_weight.shape[1]
    input_proj = proj_d[:, : 2 * R]
    output_proj = proj_d[:, 2 * R :]
    block_rows = lax.all_gather(tokens, "hid", axis=0, tiled=True)
    forward = jnp.concatenate(
        [
            project_rows(block_rows, gate_weight),
            project_rows(block_rows, up_weight),
            project_rows(block_rows, input_proj),
        ],
        axis=1,
    )
    block_rows = lax.all_gather(out_grad, "hid", axis=0, tiled=True)
    spread = lax.dot_general(
        block_rows, down_weight, (((1,), (1,)), ((), ())), preferred_element_type=jnp.float32
    )
    backward = jnp.concatenate([spread, project_rows(block_rows, output_proj)], axis=1)
    forward = lax.psum(forward, "mod")
    backward = lax.psum(backward, "mod")
    gate_act = forward[:, :width]
    up_act = forward[:, width : 2 * width]
    input_gate = forward[:, 2 * width : 2 * width + R]
    input_up = forward[:, 2 * width + R :]
    hidden_grad = backward[:, :width]
    output_down = backward[:, width:]
    hidden, gate_grad, up_grad = pointwise(gate_act, up_act, hidden_grad)
    output_gate = project_rows(gate_grad, proj_ff[:, :R])
    output_up = project_rows(up_grad, proj_ff[:, R : 2 * R])
    input_down = project_rows(hidden, proj_ff[:, 2 * R :])
    shares = R // lax.axis_size("hid")
    offset = lax.axis_index("hid") * shares
    output_gate, output_up, input_down = lax.psum((output_gate, output_up, input_down), "hid")
    own_gate = lax.dynamic_slice_in_dim(output_gate, offset, shares, 1)
    own_up = lax.dynamic_slice_in_dim(output_up, offset, shares, 1)
    own_down = lax.dynamic_slice_in_dim(output_down, offset, shares, 1)
    outputs = jnp.stack([own_gate, own_up, own_down], axis=2)
    inputs = jnp.stack([input_gate, input_up, input_down], axis=1)
    total_rows = outputs.shape[0]
    outer = (outputs[:, :, :, None] * inputs[:, None, :, :]).reshape(total_rows, shares * 3 * R)
    examples = example_ids.shape[0] // EX_TOK
    member = (example_ids[None, :] == jnp.arange(examples, dtype=jnp.int32)[:, None]).astype(
        jnp.float32
    )
    features = jnp.dot(member, outer, precision=HIGH, preferred_element_type=jnp.float32)
    partial_scores = jnp.dot(
        features,
        test_features.astype(jnp.float32).T,
        precision=HIGH,
        preferred_element_type=jnp.float32,
    )
    scores = lax.psum(partial_scores, "hid")
    return (features, scores)


def pointwise(gate_act, up_act, hidden_grad):
    sig = jax.nn.sigmoid(gate_act)
    hidden = (gate_act * sig * up_act).astype(jnp.bfloat16)
    gate_grad = (hidden_grad * up_act * sig * (1.0 + gate_act * (1.0 - sig))).astype(jnp.bfloat16)
    up_grad = (hidden_grad * gate_act * sig).astype(jnp.bfloat16)
    return hidden, gate_grad, up_grad


def ring_device(position, core, chips):
    height = chips // 2
    if isinstance(position, int):
        back = position >= height
        z = 2 * height - 1 - position if back else position
        return z * 4 + int(back) * 2 + core
    back = (position >= height).astype(jnp.int32)
    z = position + back * (2 * height - 1 - 2 * position)
    return z * 4 + back * 2 + core


def ring_position(device, chips):
    z, x = device // 4, (device // 2) % 2
    return z + x * (chips - 1 - 2 * z)


def ring_step(block, chips, step):
    pairs = [
        (ring_device(r, core, chips), ring_device((r + step) % chips, core, chips))
        for r in range(chips)
        for core in range(2)
    ]
    return lax.ppermute(block, "hid", pairs)


def core_swap(block, chips):
    return lax.ppermute(block, "hid", [(h, h ^ 1) for h in range(2 * chips)])


def gather_blocks(own, chips):
    half = own.shape[1] // 2
    found = [(0, 0, own)]
    ahead, behind = own, own
    for step in range(1, chips // 2):
        ahead = ring_step(ahead, chips, 1)
        behind = ring_step(behind, chips, -1)
        found += [(-step, 0, ahead), (step, 0, behind)]
    across = chips // 2
    found.append((across, 0, ring_step(ahead[:, :half], chips, 1)))
    found.append((across, half, ring_step(behind[:, half:], chips, -1)))
    places, blocks = [], []
    for offset, column, block in found:
        for other in range(2):
            places.append((offset, other, column))
            blocks.append(core_swap(block, chips) if other else block)
    return places, blocks


def assemble(places, chips, blocks, whole, sems):
    device = lax.axis_index("hid")
    position, core = ring_position(device, chips), device % 2
    copies = []
    for index, (offset, other, column) in enumerate(places):
        rows, columns = blocks[index].shape
        source_core = core + other - 2 * core * other
        source = ring_device((position + offset + chips) % chips, source_core, chips)
        start = pl.multiple_of(source * rows, rows)
        target = whole.at[pl.ds(start, rows), pl.ds(column, columns)]
        copies.append(pltpu.make_async_copy(blocks[index], target, sems.at[index]))
    for copy in copies:
        copy.start()
    for copy in copies:
        copy.wait()


def deep_dot(left, right, transposed, columns):
    depth = left.shape[1]
    total = jnp.zeros((left.shape[0], columns), jnp.float32)
    for start in range(0, depth, DEPTH):
        part = pl.ds(start, DEPTH)
        a = left[:, part]
        if transposed:
            total += last_dot(a, right[:, part])
        else:
            total += jnp.dot(a, right[part, :], preferred_element_type=jnp.float32)
    return total


def last_dot(a, b):
    return lax.dot_general(a, b, (((1,), (1,)), ((), ())), preferred_element_type=jnp.float32)


def forward_kernel(places, chips, *refs):
    count = len(places)
    blocks, refs = refs[:count], refs[count:]
    weight, proj = refs[0], refs[1] if len(refs) == 6 else None
    out, whole, sems = refs[-4 if proj is not None else -3], refs[-2], refs[-1]

    @pl.when(pl.program_id(0) == 0)
    def _():
        assemble(places, chips, blocks, whole, sems)
        if proj is not None:
            total = jnp.zeros(refs[3].shape, jnp.float32)
            for start in range(0, whole.shape[1], DEPTH):
                part = pl.ds(start, DEPTH)
                total += last_dot(proj[: 2 * R, part], whole[:, part])
            refs[3][...] = total

    out[...] = deep_dot(whole, weight, False, out.shape[0]).T


def forward(places, chips, blocks, weight, tile, first, tiles, proj=None):
    rows = blocks[0].shape[0] * chips * 2
    depth = weight.shape[0]
    in_specs = [pl.BlockSpec(memory_space=pl.ANY)] * len(blocks)
    in_specs.append(pl.BlockSpec((depth, tile), lambda n: (0, n + first)))
    out_shape = [jax.ShapeDtypeStruct((tiles * tile, rows), jnp.float32)]
    out_specs = [pl.BlockSpec((tile, rows), lambda n: (n, 0))]
    operands = [*blocks, weight]
    if proj is not None:
        in_specs.append(pl.BlockSpec((3 * R, depth), lambda n: (0, 0)))
        out_shape.append(jax.ShapeDtypeStruct((2 * R, rows), jnp.float32))
        out_specs.append(pl.BlockSpec((2 * R, rows), lambda n: (0, 0)))
        operands.append(proj)
    return pl.pallas_call(
        functools.partial(forward_kernel, places, chips),
        grid=(tiles,),
        out_shape=out_shape,
        in_specs=in_specs,
        out_specs=out_specs,
        scratch_shapes=[
            pltpu.VMEM((rows, depth), jnp.bfloat16),
            pltpu.SemaphoreType.DMA((len(blocks),)),
        ],
        compiler_params=pltpu.CompilerParams(vmem_limit_bytes=VMEM),
        cost_estimate=pl.CostEstimate(
            flops=4 * rows * depth * tiles * tile,
            bytes_accessed=2 * depth * tiles * tile,
            transcendentals=0,
        ),
    )(*operands)


def membership(ids, examples):
    rows = lax.broadcasted_iota(jnp.int32, (examples, ids.shape[1]), 0)
    return (jnp.broadcast_to(ids, rows.shape) == rows).astype(jnp.float32)


def exact_dot(a, b, contract):
    return lax.dot_general(
        a, b, (contract, ((), ())), precision=HIGH, preferred_element_type=jnp.float32
    )


def backward_kernel(places, chips, examples, tile, parts, *refs):
    count = len(places)
    blocks, refs = refs[:count], refs[count:]
    weight, proj, proj_ff, ids = refs[:4]
    gates, ups = refs[4 : 4 + parts], refs[4 + parts : 4 + 2 * parts]
    sends, (whole, spread, flipped, sums, ready, sems) = refs[4 + 2 * parts : -6], refs[-6:]
    step = pl.program_id(0)
    hid = 2 * chips
    shares = R // hid
    near = len(sends)

    @pl.when(step == 0)
    def _():
        assemble(places, chips, blocks, whole, sems)
        spread[...] = jnp.zeros_like(spread)
        flipped[...] = jnp.zeros_like(flipped)

    depth = weight.shape[1]
    x = whole[:, pl.ds(pl.multiple_of(step * depth, depth), depth)]
    spread[...] += last_dot(weight[...], x)
    turned = last_dot(proj[2 * R :, :], x)
    for lanes in range(flipped.shape[0]):
        flipped[lanes] += turned[:, lanes * 128 : (lanes + 1) * 128]

    @pl.when(step == pl.num_programs(0) - 1)
    def _():
        sums[...] = jnp.zeros_like(sums)
        start = 0
        for gate, up in zip(gates, ups):
            for local in range(0, gate.shape[0], tile):
                part = pl.ds(local, tile)
                hidden, gate_grad, up_grad = pointwise(
                    gate[part, :], up[part, :], spread[start : start + tile, :]
                )
                for m, value in enumerate((gate_grad, up_grad, hidden)):
                    sums[m * R : (m + 1) * R, :] += jnp.dot(
                        proj_ff[m * R : (m + 1) * R, start : start + tile],
                        value,
                        preferred_element_type=jnp.float32,
                    )
                start += tile
        for m in range(2):
            for p in range(hid):
                own = sums[m * R + p * shares : m * R + (p + 1) * shares, :]
                ready[p, m * shares : (m + 1) * shares, :] = own
        member = membership(ids[...], examples)
        total_rows = member.shape[1]
        for j in range(shares):
            every = pl.ds(j, hid, shares)
            own = jnp.concatenate([flipped[k, every, :] for k in range(flipped.shape[0])], axis=1)
            left = (own[:, None, :] * member[None, :, :]).reshape(hid * examples, total_rows)
            product = exact_dot(left, sums[2 * R :, :], ((1,), (1,)))
            ready[:, 2 * shares :, j * R : (j + 1) * R] = product.reshape(hid, examples, R)
        mine = lax.rem(lax.axis_index("hid"), near)
        for d in range(near):
            partner = mine + d - 2 * (mine & d)
            for z in range(hid // near):
                sends[d][z] = ready[z * near + partner]


def backward(places, chips, blocks, weight, gates, ups, proj, proj_ff, ids, depth_tile, tile):
    rows = blocks[0].shape[0] * chips * 2
    width, depth = weight.shape
    hid = 2 * chips
    shares, examples = R // hid, rows // EX_TOK
    deep = 2 * shares + examples

    def stay(*shape):
        return pl.BlockSpec(shape, lambda k: (0,) * len(shape))

    return pl.pallas_call(
        functools.partial(backward_kernel, places, chips, examples, tile, len(gates)),
        grid=(depth // depth_tile,),
        out_shape=[jax.ShapeDtypeStruct((hid // NEAR, deep, rows), jnp.float32)] * NEAR,
        in_specs=[pl.BlockSpec(memory_space=pl.ANY)] * len(blocks)
        + [
            pl.BlockSpec((width, depth_tile), lambda k: (0, k)),
            pl.BlockSpec((3 * R, depth_tile), lambda k: (0, k)),
            stay(3 * R, width),
            stay(1, rows),
        ]
        + [stay(*value.shape) for value in (*gates, *ups)],
        out_specs=[stay(hid // NEAR, deep, rows)] * NEAR,
        scratch_shapes=[
            pltpu.VMEM((rows, depth), jnp.bfloat16),
            pltpu.VMEM((width, rows), jnp.float32),
            pltpu.VMEM((rows // 128, R, 128), jnp.float32),
            pltpu.VMEM((3 * R, rows), jnp.float32),
            pltpu.VMEM((hid, deep, rows), jnp.float32),
            pltpu.SemaphoreType.DMA((len(blocks),)),
        ],
        compiler_params=pltpu.CompilerParams(vmem_limit_bytes=VMEM),
        cost_estimate=pl.CostEstimate(
            flops=2 * rows * depth * width, bytes_accessed=2 * depth * width, transcendentals=0
        ),
    )(*blocks, weight, proj, proj_ff, ids, *gates, *ups)


def exchange_near(sends):
    hid = lax.axis_size("hid")
    return [sends[0]] + [
        lax.ppermute(sends[d], "hid", [(h, h ^ d) for h in range(hid)]) for d in range(1, NEAR)
    ]


def exchange_far(sends):
    hid = lax.axis_size("hid")
    return [sends[0]] + [
        lax.ppermute(sends[e], "hid", [(h, h ^ (e * NEAR)) for h in range(hid)])
        for e in range(1, hid // NEAR)
    ]


def combine_kernel(count, *refs):
    parts, sends = refs[:count], refs[count:]
    mine = lax.axis_index("hid") // NEAR
    for e in range(len(sends)):
        partner = mine + e - 2 * (mine & e)
        sends[e][...] = sum(part[partner] for part in parts[1:]) + parts[0][partner]


def combine(parts):
    far = parts[0].shape[0]
    vmem = pl.BlockSpec(memory_space=pltpu.VMEM)
    return pl.pallas_call(
        functools.partial(combine_kernel, len(parts)),
        out_shape=[jax.ShapeDtypeStruct(parts[0].shape[1:], jnp.float32)] * far,
        in_specs=[vmem] * len(parts),
        out_specs=[vmem] * far,
        compiler_params=pltpu.CompilerParams(vmem_limit_bytes=VMEM),
    )(*parts)


def features_kernel(hid, count, *refs):
    received, (inputs, ids, tests, features, partial) = refs[:count], refs[count:]
    shares = R // hid
    examples = features.shape[0]
    member = membership(ids[...], examples)
    total = sum(part[...] for part in received[1:]) + received[0][...]
    for m in range(2):
        own = total[m * shares : (m + 1) * shares]
        left = (own[:, None, :] * member[None, :, :]).reshape(shares * examples, own.shape[1])
        product = exact_dot(left, inputs[m * R : (m + 1) * R, :], ((1,), (1,)))
        for j in range(shares):
            start = (j * 3 + m) * R
            features[:, start : start + R] = product[j * examples : (j + 1) * examples]
    for j in range(shares):
        start = (j * 3 + 2) * R
        features[:, start : start + R] = total[2 * shares :, j * R : (j + 1) * R]
    partial[...] = exact_dot(features[...], tests[...].astype(jnp.float32), ((1,), (1,)))


def finish(hid, received, inputs, ids, tests):
    examples = ids.shape[1] // EX_TOK
    vmem = pl.BlockSpec(memory_space=pltpu.VMEM)
    return pl.pallas_call(
        functools.partial(features_kernel, hid, len(received)),
        out_shape=(
            jax.ShapeDtypeStruct((examples, tests.shape[1]), jnp.float32),
            jax.ShapeDtypeStruct((examples, tests.shape[0]), jnp.float32),
        ),
        in_specs=[vmem] * (len(received) + 3),
        out_specs=(vmem, vmem),
        compiler_params=pltpu.CompilerParams(vmem_limit_bytes=VMEM),
    )(*received, inputs, ids, tests)


def local_ring(
    tokens,
    out_grad,
    gate_weight,
    up_weight,
    down_weight,
    proj_d,
    proj_ff,
    example_ids,
    test_features,
):
    chips = lax.axis_size("hid") // 2
    ids = example_ids[None, :]
    places, token_blocks = gather_blocks(tokens, chips)
    _, grad_blocks = gather_blocks(out_grad, chips)
    tiles = gate_weight.shape[1] // TILE
    gate, inputs = forward(places, chips, token_blocks, gate_weight, TILE, 0, tiles, proj_d.T)
    (up,) = forward(places, chips, token_blocks, up_weight, TILE, 0, tiles)
    sends = backward(
        places, chips, grad_blocks, down_weight, [gate], [up], proj_d.T, proj_ff.T, ids, 1024, TILE
    )
    received = exchange_far(combine(exchange_near(sends)))
    features, partial = finish(2 * chips, received, inputs, ids, test_features)
    near = sum(exchange_near([partial] * NEAR))
    scores = sum(exchange_far([near] * (2 * chips // NEAR)))
    return features, scores


def solution(mesh):
    one_ring = mesh.shape["mod"] == 1 and mesh.shape["hid"] <= 16
    return jax.shard_map(
        local_ring if one_ring else local_general,
        mesh=mesh,
        in_specs=(
            P(("groups", "hid"), "mod"),
            P(("groups", "hid"), "mod"),
            P("mod", "hid"),
            P("mod", "hid"),
            P("hid", "mod"),
            P("mod", None),
            P("hid", None),
            P("groups"),
            P("groups", "hid"),
        ),
        out_specs=(P("groups", "hid"), P("groups", None)),
        check_vma=False,
    )
```

```python
import functools

import jax
import jax.numpy as jnp
from jax import lax
from jax.experimental import pallas as pl
from jax.experimental.pallas import tpu as pltpu
from jax.sharding import PartitionSpec as P

R = 64
EX_TOK = 32
TILE = 256
DEPTH = 2048
SPLIT = 4
VMEM = 56 * 1024 * 1024
HIGH = lax.Precision.HIGHEST


def project_rows(block_rows, weights):
    return jnp.dot(block_rows, weights, preferred_element_type=jnp.float32)


def local_general(
    tokens,
    out_grad,
    gate_weight,
    up_weight,
    down_weight,
    proj_d,
    proj_ff,
    example_ids,
    test_features,
):
    width = gate_weight.shape[1]
    input_proj = proj_d[:, : 2 * R]
    output_proj = proj_d[:, 2 * R :]
    block_rows = lax.all_gather(tokens, "hid", axis=0, tiled=True)
    forward = jnp.concatenate(
        [
            project_rows(block_rows, gate_weight),
            project_rows(block_rows, up_weight),
            project_rows(block_rows, input_proj),
        ],
        axis=1,
    )
    block_rows = lax.all_gather(out_grad, "hid", axis=0, tiled=True)
    spread = lax.dot_general(
        block_rows, down_weight, (((1,), (1,)), ((), ())), preferred_element_type=jnp.float32
    )
    backward = jnp.concatenate([spread, project_rows(block_rows, output_proj)], axis=1)
    forward = lax.psum(forward, "mod")
    backward = lax.psum(backward, "mod")
    gate_act = forward[:, :width]
    up_act = forward[:, width : 2 * width]
    input_gate = forward[:, 2 * width : 2 * width + R]
    input_up = forward[:, 2 * width + R :]
    hidden_grad = backward[:, :width]
    output_down = backward[:, width:]
    hidden, gate_grad, up_grad = pointwise(gate_act, up_act, hidden_grad)
    output_gate = project_rows(gate_grad, proj_ff[:, :R])
    output_up = project_rows(up_grad, proj_ff[:, R : 2 * R])
    input_down = project_rows(hidden, proj_ff[:, 2 * R :])
    shares = R // lax.axis_size("hid")
    offset = lax.axis_index("hid") * shares
    output_gate, output_up, input_down = lax.psum((output_gate, output_up, input_down), "hid")
    own_gate = lax.dynamic_slice_in_dim(output_gate, offset, shares, 1)
    own_up = lax.dynamic_slice_in_dim(output_up, offset, shares, 1)
    own_down = lax.dynamic_slice_in_dim(output_down, offset, shares, 1)
    outputs = jnp.stack([own_gate, own_up, own_down], axis=2)
    inputs = jnp.stack([input_gate, input_up, input_down], axis=1)
    total_rows = outputs.shape[0]
    outer = (outputs[:, :, :, None] * inputs[:, None, :, :]).reshape(total_rows, shares * 3 * R)
    examples = example_ids.shape[0] // EX_TOK
    member = (example_ids[None, :] == jnp.arange(examples, dtype=jnp.int32)[:, None]).astype(
        jnp.float32
    )
    features = jnp.dot(member, outer, precision=HIGH, preferred_element_type=jnp.float32)
    partial_scores = jnp.dot(
        features,
        test_features.astype(jnp.float32).T,
        precision=HIGH,
        preferred_element_type=jnp.float32,
    )
    scores = lax.psum(partial_scores, "hid")
    return (features, scores)


def pointwise(gate_act, up_act, hidden_grad):
    sig = jax.nn.sigmoid(gate_act)
    hidden = (gate_act * sig * up_act).astype(jnp.bfloat16)
    gate_grad = (hidden_grad * up_act * sig * (1.0 + gate_act * (1.0 - sig))).astype(jnp.bfloat16)
    up_grad = (hidden_grad * gate_act * sig).astype(jnp.bfloat16)
    return hidden, gate_grad, up_grad


def ring_device(position, core, chips):
    height = chips // 2
    if isinstance(position, int):
        back = position >= height
        z = 2 * height - 1 - position if back else position
        return z * 4 + int(back) * 2 + core
    back = (position >= height).astype(jnp.int32)
    z = position + back * (2 * height - 1 - 2 * position)
    return z * 4 + back * 2 + core


def ring_position(device, chips):
    z, x = device // 4, (device // 2) % 2
    return z + x * (chips - 1 - 2 * z)


def ring_step(block, chips, step):
    pairs = [
        (ring_device(r, core, chips), ring_device((r + step) % chips, core, chips))
        for r in range(chips)
        for core in range(2)
    ]
    return lax.ppermute(block, "hid", pairs)


def core_swap(block, chips):
    return lax.ppermute(block, "hid", [(h, h ^ 1) for h in range(2 * chips)])


def gather_blocks(own, chips, base=0):
    half = own.shape[1] // 2
    places, blocks, steps = [], [], []

    def found(offset, column, block):
        for other in range(2):
            places.append((offset, other, base + column))
            blocks.append(core_swap(block, chips) if other else block)

    found(0, 0, own)
    ahead, behind = own, own
    for step in range(1, chips // 2):
        ahead = ring_step(ahead, chips, 1)
        behind = ring_step(behind, chips, -1)
        found(-step, 0, ahead)
        found(step, 0, behind)
        steps.append((ahead, behind))
    across = chips // 2
    found(across, 0, ring_step(ahead[:, :half], chips, 1))
    found(across, half, ring_step(behind[:, half:], chips, -1))
    return places, blocks, steps


def after(value, *others):
    return lax.optimization_barrier((value, *others))[0]


def assemble(places, chips, blocks, whole, sems):
    device = lax.axis_index("hid")
    position, core = ring_position(device, chips), device % 2
    copies = []
    for index, (offset, other, column) in enumerate(places):
        rows, columns = blocks[index].shape
        source_core = core + other - 2 * core * other
        source = ring_device((position + offset + chips) % chips, source_core, chips)
        start = pl.multiple_of(source * rows, rows)
        target = whole.at[pl.ds(start, rows), pl.ds(column, columns)]
        copies.append(pltpu.make_async_copy(blocks[index], target, sems.at[index]))
    for copy in copies:
        copy.start()
    for copy in copies:
        copy.wait()


def last_dot(a, b):
    return lax.dot_general(a, b, (((1,), (1,)), ((), ())), preferred_element_type=jnp.float32)


def deep_dot(left, rights):
    total, start = None, 0
    for right in rights:
        part = pl.ds(start, right.shape[0])
        term = jnp.dot(left[:, part], right[...], preferred_element_type=jnp.float32)
        total = term if total is None else total + term
        start += right.shape[0]
    return total


def forward_kernel(places, chips, *refs):
    count = len(places)
    blocks, refs = refs[:count], refs[count:]
    (gate, up, whole, sems), weights = refs[-4:], refs[: 2 * SPLIT]

    @pl.when(pl.program_id(0) == 0)
    def _():
        assemble(places, chips, blocks, whole, sems)

    gate[...] = deep_dot(whole, weights[:SPLIT]).T
    up[...] = deep_dot(whole, weights[SPLIT:]).T


def forward(places, chips, blocks, gate_weight, up_weight, tile, first, tiles, waits):
    depth = gate_weight.shape[0]
    rows = blocks[0].shape[0] * chips * 2
    return pl.pallas_call(
        functools.partial(forward_kernel, places, chips),
        grid=(tiles,),
        out_shape=[jax.ShapeDtypeStruct((tiles * tile, rows), jnp.float32)] * 2,
        in_specs=[pl.BlockSpec(memory_space=pl.ANY)] * len(blocks)
        + [
            pl.BlockSpec((depth // SPLIT, tile), lambda n, q=q: (q, n + first))
            for q in range(SPLIT)
        ]
        * 2
        + [pl.BlockSpec(memory_space=pl.ANY)] * len(waits),
        out_specs=[pl.BlockSpec((tile, rows), lambda n: (n, 0))] * 2,
        scratch_shapes=[
            pltpu.VMEM((rows, depth), jnp.bfloat16),
            pltpu.SemaphoreType.DMA((len(blocks),)),
        ],
        compiler_params=pltpu.CompilerParams(vmem_limit_bytes=VMEM),
        cost_estimate=pl.CostEstimate(
            flops=8 * rows * depth * tiles * tile,
            bytes_accessed=8 * depth * tiles * tile,
            transcendentals=0,
        ),
    )(*blocks, *[gate_weight] * SPLIT, *[up_weight] * SPLIT, *waits)


def inputs_kernel(places, chips, *refs):
    count = len(places)
    blocks, (proj, out, whole, sems) = refs[:count], refs[count:]
    assemble(places, chips, blocks, whole, sems)
    total = jnp.zeros(out.shape, jnp.float32)
    for start in range(0, whole.shape[1], DEPTH):
        part = pl.ds(start, DEPTH)
        total += last_dot(proj[: 2 * R, part], whole[:, part])
    out[...] = total


def project_inputs(places, chips, blocks, proj):
    rows, depth = blocks[0].shape[0] * chips * 2, proj.shape[1]
    vmem = pl.BlockSpec(memory_space=pltpu.VMEM)
    return pl.pallas_call(
        functools.partial(inputs_kernel, places, chips),
        out_shape=jax.ShapeDtypeStruct((2 * R, rows), jnp.float32),
        in_specs=[pl.BlockSpec(memory_space=pl.ANY)] * len(blocks) + [vmem],
        out_specs=vmem,
        scratch_shapes=[
            pltpu.VMEM((rows, depth), jnp.bfloat16),
            pltpu.SemaphoreType.DMA((len(blocks),)),
        ],
        compiler_params=pltpu.CompilerParams(vmem_limit_bytes=VMEM),
        cost_estimate=pl.CostEstimate(
            flops=16 * R * rows * depth, bytes_accessed=8 * R * depth, transcendentals=0
        ),
    )(*blocks, proj)


def membership(ids, examples):
    rows = lax.broadcasted_iota(jnp.int32, (examples, ids.shape[1]), 0)
    return (jnp.broadcast_to(ids, rows.shape) == rows).astype(jnp.float32)


def exact_dot(a, b, contract):
    return lax.dot_general(
        a, b, (contract, ((), ())), precision=HIGH, preferred_element_type=jnp.float32
    )


def backward_kernel(places, chips, examples, tile, parts, *refs):
    count = len(places)
    blocks, refs = refs[:count], refs[count:]
    weights, refs = refs[:SPLIT], refs[SPLIT:]
    proj, proj_ff, ids = refs[:3]
    gates, ups = refs[3 : 3 + parts], refs[3 + parts : 3 + 2 * parts]
    ready, whole, spread, flipped, sums, sems = refs[3 + 2 * parts :]
    step = pl.program_id(0)
    hid = 2 * chips
    shares = R // hid

    @pl.when(step == 0)
    def _():
        assemble(places, chips, blocks, whole, sems)
        spread[...] = jnp.zeros_like(spread)
        flipped[...] = jnp.zeros_like(flipped)

    height, depth = weights[0].shape
    x = whole[:, pl.ds(pl.multiple_of(step * depth, depth), depth)]
    for q, weight in enumerate(weights):
        spread[q * height : (q + 1) * height, :] += last_dot(weight[...], x)
    turned = last_dot(proj[2 * R :, :], x)
    for lanes in range(flipped.shape[0]):
        flipped[lanes] += turned[:, lanes * 128 : (lanes + 1) * 128]

    @pl.when(step == pl.num_programs(0) - 1)
    def _():
        sums[...] = jnp.zeros_like(sums)
        start = 0
        for gate, up in zip(gates, ups):
            for local in range(0, gate.shape[0], tile):
                part = pl.ds(local, tile)
                hidden, gate_grad, up_grad = pointwise(
                    gate[part, :], up[part, :], spread[start : start + tile, :]
                )
                for m, value in enumerate((gate_grad, up_grad, hidden)):
                    sums[m * R : (m + 1) * R, :] += jnp.dot(
                        proj_ff[m * R : (m + 1) * R, start : start + tile],
                        value,
                        preferred_element_type=jnp.float32,
                    )
                start += tile
        for m in range(2):
            for p in range(hid):
                own = sums[m * R + p * shares : m * R + (p + 1) * shares, :]
                ready[p, m * shares : (m + 1) * shares, :] = own
        member = membership(ids[...], examples)
        total_rows = member.shape[1]
        for j in range(shares):
            every = pl.ds(j, hid, shares)
            own = jnp.concatenate([flipped[k, every, :] for k in range(flipped.shape[0])], axis=1)
            left = (own[:, None, :] * member[None, :, :]).reshape(hid * examples, total_rows)
            product = exact_dot(left, sums[2 * R :, :], ((1,), (1,)))
            ready[:, 2 * shares :, j * R : (j + 1) * R] = product.reshape(hid, examples, R)


def backward(places, chips, blocks, weight, gates, ups, proj, proj_ff, ids, depth_tile, tile):
    rows = blocks[0].shape[0] * chips * 2
    width, depth = weight.shape
    hid = 2 * chips
    shares, examples = R // hid, rows // EX_TOK
    deep = 2 * shares + examples

    def stay(*shape):
        return pl.BlockSpec(shape, lambda k: (0,) * len(shape))

    return pl.pallas_call(
        functools.partial(backward_kernel, places, chips, examples, tile, len(gates)),
        grid=(depth // depth_tile,),
        out_shape=jax.ShapeDtypeStruct((hid, deep, rows), jnp.float32),
        in_specs=[pl.BlockSpec(memory_space=pl.ANY)] * len(blocks)
        + [
            pl.BlockSpec((width // SPLIT, depth_tile), lambda k, q=q: (q, k))
            for q in range(SPLIT)
        ]
        + [
            pl.BlockSpec((3 * R, depth_tile), lambda k: (0, k)),
            stay(3 * R, width),
            stay(1, rows),
        ]
        + [stay(*value.shape) for value in (*gates, *ups)],
        out_specs=stay(hid, deep, rows),
        scratch_shapes=[
            pltpu.VMEM((rows, depth), jnp.bfloat16),
            pltpu.VMEM((width, rows), jnp.float32),
            pltpu.VMEM((rows // 128, R, 128), jnp.float32),
            pltpu.VMEM((3 * R, rows), jnp.float32),
            pltpu.SemaphoreType.DMA((len(blocks),)),
        ],
        compiler_params=pltpu.CompilerParams(vmem_limit_bytes=VMEM),
        cost_estimate=pl.CostEstimate(
            flops=2 * rows * depth * width, bytes_accessed=2 * depth * width, transcendentals=0
        ),
    )(*blocks, *[weight] * SPLIT, proj, proj_ff, ids, *gates, *ups)


def features_kernel(hid, received, inputs, ids, tests, features, partial):
    shares = R // hid
    examples = features.shape[0]
    member = membership(ids[...], examples)
    total = jnp.sum(received[...], axis=0)
    for m in range(2):
        own = total[m * shares : (m + 1) * shares]
        left = (own[:, None, :] * member[None, :, :]).reshape(shares * examples, own.shape[1])
        product = exact_dot(left, inputs[m * R : (m + 1) * R, :], ((1,), (1,)))
        for j in range(shares):
            start = (j * 3 + m) * R
            features[:, start : start + R] = product[j * examples : (j + 1) * examples]
    for j in range(shares):
        start = (j * 3 + 2) * R
        features[:, start : start + R] = total[2 * shares :, j * R : (j + 1) * R]
    scores = exact_dot(features[...], tests[...].astype(jnp.float32), ((1,), (1,)))
    partial[...] = jnp.broadcast_to(scores[None], partial.shape)


def finish(received, inputs, ids, tests):
    hid = received.shape[0]
    examples = ids.shape[1] // EX_TOK
    vmem = pl.BlockSpec(memory_space=pltpu.VMEM)
    return pl.pallas_call(
        functools.partial(features_kernel, hid),
        out_shape=(
            jax.ShapeDtypeStruct((examples, tests.shape[1]), jnp.float32),
            jax.ShapeDtypeStruct((hid, examples, tests.shape[0]), jnp.float32),
        ),
        in_specs=[vmem] * 4,
        out_specs=(vmem, vmem),
        compiler_params=pltpu.CompilerParams(vmem_limit_bytes=VMEM),
    )(received, inputs, ids, tests)


def local_ring(
    tokens,
    out_grad,
    gate_weight,
    up_weight,
    down_weight,
    proj_d,
    proj_ff,
    example_ids,
    test_features,
):
    chips = lax.axis_size("hid") // 2
    ids = example_ids[None, :]
    half = tokens.shape[1] // 2
    places, token_blocks, _ = gather_blocks(tokens[:, :half], chips)
    more_places, more_blocks, steps = gather_blocks(tokens[:, half:], chips, half)
    places, token_blocks = places + more_places, token_blocks + more_blocks
    grad_places, grad_blocks, grad_steps = gather_blocks(after(out_grad, *steps[-1]), chips)
    tiles = gate_weight.shape[1] // TILE
    shares = -(-tiles // len(grad_steps))
    gates, ups = [], []
    for index, first in enumerate(range(0, tiles, shares)):
        gate, up = forward(
            places,
            chips,
            token_blocks,
            gate_weight,
            up_weight,
            TILE,
            first,
            min(shares, tiles - first),
            grad_steps[index],
        )
        gates.append(gate)
        ups.append(up)
    send = backward(
        grad_places, chips, grad_blocks, down_weight, gates, ups, proj_d.T, proj_ff.T, ids, 1024, TILE
    )
    received = lax.all_to_all(send, "hid", 0, 0)
    inputs = project_inputs(places, chips, token_blocks, proj_d.T)
    features, partial = finish(received, inputs, ids, test_features)
    scores = jnp.sum(lax.all_to_all(partial, "hid", 0, 0), axis=0)
    return features, scores


def solution(mesh):
    one_ring = mesh.shape["mod"] == 1 and mesh.shape["hid"] <= 16
    return jax.shard_map(
        local_ring if one_ring else local_general,
        mesh=mesh,
        in_specs=(
            P(("groups", "hid"), "mod"),
            P(("groups", "hid"), "mod"),
            P("mod", "hid"),
            P("mod", "hid"),
            P("hid", "mod"),
            P("mod", None),
            P("hid", None),
            P("groups"),
            P("groups", "hid"),
        ),
        out_specs=(P("groups", "hid"), P("groups", None)),
        check_vma=False,
    )
```

```python
import functools

import jax
import jax.numpy as jnp
from jax import lax
from jax.experimental import pallas as pl
from jax.experimental.pallas import tpu as pltpu
from jax.sharding import PartitionSpec as P

R = 64
EX_TOK = 32
TILE = 256
DEPTH = 2048
SPLIT = 4
MEBI = 1024 * 1024
HIGH = lax.Precision.HIGHEST


def project_rows(block_rows, weights):
    return jnp.dot(block_rows, weights, preferred_element_type=jnp.float32)


def local_general(
    tokens,
    out_grad,
    gate_weight,
    up_weight,
    down_weight,
    proj_d,
    proj_ff,
    example_ids,
    test_features,
):
    width = gate_weight.shape[1]
    input_proj = proj_d[:, : 2 * R]
    output_proj = proj_d[:, 2 * R :]
    block_rows = lax.all_gather(tokens, "hid", axis=0, tiled=True)
    forward = jnp.concatenate(
        [
            project_rows(block_rows, gate_weight),
            project_rows(block_rows, up_weight),
            project_rows(block_rows, input_proj),
        ],
        axis=1,
    )
    block_rows = lax.all_gather(out_grad, "hid", axis=0, tiled=True)
    spread = lax.dot_general(
        block_rows, down_weight, (((1,), (1,)), ((), ())), preferred_element_type=jnp.float32
    )
    backward = jnp.concatenate([spread, project_rows(block_rows, output_proj)], axis=1)
    forward = lax.psum(forward, "mod")
    backward = lax.psum(backward, "mod")
    gate_act = forward[:, :width]
    up_act = forward[:, width : 2 * width]
    input_gate = forward[:, 2 * width : 2 * width + R]
    input_up = forward[:, 2 * width + R :]
    hidden_grad = backward[:, :width]
    output_down = backward[:, width:]
    hidden, gate_grad, up_grad = pointwise(gate_act, up_act, hidden_grad)
    output_gate = project_rows(gate_grad, proj_ff[:, :R])
    output_up = project_rows(up_grad, proj_ff[:, R : 2 * R])
    input_down = project_rows(hidden, proj_ff[:, 2 * R :])
    shares = R // lax.axis_size("hid")
    offset = lax.axis_index("hid") * shares
    output_gate, output_up, input_down = lax.psum((output_gate, output_up, input_down), "hid")
    own_gate = lax.dynamic_slice_in_dim(output_gate, offset, shares, 1)
    own_up = lax.dynamic_slice_in_dim(output_up, offset, shares, 1)
    own_down = lax.dynamic_slice_in_dim(output_down, offset, shares, 1)
    outputs = jnp.stack([own_gate, own_up, own_down], axis=2)
    inputs = jnp.stack([input_gate, input_up, input_down], axis=1)
    total_rows = outputs.shape[0]
    outer = (outputs[:, :, :, None] * inputs[:, None, :, :]).reshape(total_rows, shares * 3 * R)
    examples = example_ids.shape[0] // EX_TOK
    member = (example_ids[None, :] == jnp.arange(examples, dtype=jnp.int32)[:, None]).astype(
        jnp.float32
    )
    features = jnp.dot(member, outer, precision=HIGH, preferred_element_type=jnp.float32)
    partial_scores = jnp.dot(
        features,
        test_features.astype(jnp.float32).T,
        precision=HIGH,
        preferred_element_type=jnp.float32,
    )
    scores = lax.psum(partial_scores, "hid")
    return (features, scores)


def pointwise(gate_act, up_act, hidden_grad):
    sig = jax.nn.sigmoid(gate_act)
    hidden = (gate_act * sig * up_act).astype(jnp.bfloat16)
    gate_grad = (hidden_grad * up_act * sig * (1.0 + gate_act * (1.0 - sig))).astype(jnp.bfloat16)
    up_grad = (hidden_grad * gate_act * sig).astype(jnp.bfloat16)
    return hidden, gate_grad, up_grad


def ring_device(position, core, chips):
    height = chips // 2
    if isinstance(position, int):
        back = position >= height
        z = 2 * height - 1 - position if back else position
        return z * 4 + int(back) * 2 + core
    back = (position >= height).astype(jnp.int32)
    z = position + back * (2 * height - 1 - 2 * position)
    return z * 4 + back * 2 + core


def ring_position(device, chips):
    z, x = device // 4, (device // 2) % 2
    return z + x * (chips - 1 - 2 * z)


def ring_step(block, chips, step):
    pairs = [
        (ring_device(r, core, chips), ring_device((r + step) % chips, core, chips))
        for r in range(chips)
        for core in range(2)
    ]
    return lax.ppermute(block, "hid", pairs)


def core_swap(block, chips):
    return lax.ppermute(block, "hid", [(h, h ^ 1) for h in range(2 * chips)])


def gather_blocks(own, chips):
    half = own.shape[1] // 2
    places, blocks = [], []

    def found(offset, column, block):
        for other in range(2):
            places.append((offset, other, column))
            blocks.append(core_swap(block, chips) if other else block)

    found(0, 0, own)
    ahead, behind = own, own
    for step in range(1, chips // 2):
        ahead = ring_step(ahead, chips, 1)
        behind = ring_step(behind, chips, -1)
        found(-step, 0, ahead)
        found(step, 0, behind)
    across = chips // 2
    found(across, 0, ring_step(ahead[:, :half], chips, 1))
    found(across, half, ring_step(behind[:, half:], chips, -1))
    return places, blocks


def assemble(places, chips, blocks, whole, sems):
    device = lax.axis_index("hid")
    position, core = ring_position(device, chips), device % 2
    copies = []
    for index, (offset, other, column) in enumerate(places):
        rows, columns = blocks[index].shape
        source_core = core + other - 2 * core * other
        source = ring_device((position + offset + chips) % chips, source_core, chips)
        start = pl.multiple_of(source * rows, rows)
        target = whole.at[pl.ds(start, rows), pl.ds(column, columns)]
        copies.append(pltpu.make_async_copy(blocks[index], target, sems.at[index]))
    for copy in copies:
        copy.start()
    for copy in copies:
        copy.wait()


def last_dot(a, b):
    return lax.dot_general(a, b, (((1,), (1,)), ((), ())), preferred_element_type=jnp.float32)


def forward_kernel(places, chips, *refs):
    count = len(places)
    blocks, refs = refs[:count], refs[count:]
    gate_weight, up_weight, gate, up, gate_sum, up_sum, whole, sems = refs
    n, k = pl.program_id(0), pl.program_id(1)

    @pl.when((n == 0) & (k == 0))
    def _():
        assemble(places, chips, blocks, whole, sems)

    depth = gate_weight.shape[0]
    x = whole[:, pl.ds(pl.multiple_of(k * depth, depth), depth)]
    gate_part = jnp.dot(x, gate_weight[...], preferred_element_type=jnp.float32)
    up_part = jnp.dot(x, up_weight[...], preferred_element_type=jnp.float32)

    @pl.when(k == 0)
    def _():
        gate_sum[...] = gate_part
        up_sum[...] = up_part

    @pl.when(k == 1)
    def _():
        gate[...] = (gate_sum[...] + gate_part).T
        up[...] = (up_sum[...] + up_part).T


def forward(places, chips, blocks, gate_weight, up_weight, tile):
    depth, width = gate_weight.shape
    rows = blocks[0].shape[0] * chips * 2
    return pl.pallas_call(
        functools.partial(forward_kernel, places, chips),
        grid=(width // tile, 2),
        out_shape=[jax.ShapeDtypeStruct((width, rows), jnp.float32)] * 2,
        in_specs=[pl.BlockSpec(memory_space=pl.ANY)] * len(blocks)
        + [pl.BlockSpec((depth // 2, tile), lambda n, k: (k, n))] * 2,
        out_specs=[pl.BlockSpec((tile, rows), lambda n, k: (n, 0))] * 2,
        scratch_shapes=[
            pltpu.VMEM((rows, tile), jnp.float32),
            pltpu.VMEM((rows, tile), jnp.float32),
            pltpu.VMEM((rows, depth), jnp.bfloat16),
            pltpu.SemaphoreType.DMA((len(blocks),)),
        ],
        compiler_params=pltpu.CompilerParams(vmem_limit_bytes=20 * MEBI),
        cost_estimate=pl.CostEstimate(
            flops=4 * rows * depth * width, bytes_accessed=4 * depth * width, transcendentals=0
        ),
    )(*blocks, gate_weight, up_weight)


def inputs_kernel(places, chips, *refs):
    count = len(places)
    blocks, (proj, out, whole, sems) = refs[:count], refs[count:]
    assemble(places, chips, blocks, whole, sems)
    total = jnp.zeros(out.shape, jnp.float32)
    for start in range(0, whole.shape[1], DEPTH):
        part = pl.ds(start, DEPTH)
        total += last_dot(proj[: 2 * R, part], whole[:, part])
    out[...] = total


def project_inputs(places, chips, blocks, proj):
    rows, depth = blocks[0].shape[0] * chips * 2, proj.shape[1]
    vmem = pl.BlockSpec(memory_space=pltpu.VMEM)
    return pl.pallas_call(
        functools.partial(inputs_kernel, places, chips),
        out_shape=jax.ShapeDtypeStruct((2 * R, rows), jnp.float32),
        in_specs=[pl.BlockSpec(memory_space=pl.ANY)] * len(blocks) + [vmem],
        out_specs=vmem,
        scratch_shapes=[
            pltpu.VMEM((rows, depth), jnp.bfloat16),
            pltpu.SemaphoreType.DMA((len(blocks),)),
        ],
        compiler_params=pltpu.CompilerParams(vmem_limit_bytes=24 * MEBI),
        cost_estimate=pl.CostEstimate(
            flops=16 * R * rows * depth, bytes_accessed=8 * R * depth, transcendentals=0
        ),
    )(*blocks, proj)


def membership(ids, examples):
    rows = lax.broadcasted_iota(jnp.int32, (examples, ids.shape[1]), 0)
    return (jnp.broadcast_to(ids, rows.shape) == rows).astype(jnp.float32)


def exact_dot(a, b, contract):
    return lax.dot_general(
        a, b, (contract, ((), ())), precision=HIGH, preferred_element_type=jnp.float32
    )


def backward_kernel(places, chips, examples, tile, parts, *refs):
    count = len(places)
    blocks, refs = refs[:count], refs[count:]
    weights, refs = refs[:SPLIT], refs[SPLIT:]
    proj, proj_ff, ids = refs[:3]
    gates, ups = refs[3 : 3 + parts], refs[3 + parts : 3 + 2 * parts]
    ready, whole, spread, flipped, sums, sems = refs[3 + 2 * parts :]
    step = pl.program_id(0)
    hid = 2 * chips
    shares = R // hid

    @pl.when(step == 0)
    def _():
        assemble(places, chips, blocks, whole, sems)
        spread[...] = jnp.zeros_like(spread)
        flipped[...] = jnp.zeros_like(flipped)

    height, depth = weights[0].shape
    x = whole[:, pl.ds(pl.multiple_of(step * depth, depth), depth)]
    for q, weight in enumerate(weights):
        spread[q * height : (q + 1) * height, :] += last_dot(weight[...], x)
    turned = last_dot(proj[2 * R :, :], x)
    for lanes in range(flipped.shape[0]):
        flipped[lanes] += turned[:, lanes * 128 : (lanes + 1) * 128]

    @pl.when(step == pl.num_programs(0) - 1)
    def _():
        sums[...] = jnp.zeros_like(sums)
        start = 0
        for gate, up in zip(gates, ups):
            for local in range(0, gate.shape[0], tile):
                part = pl.ds(local, tile)
                hidden, gate_grad, up_grad = pointwise(
                    gate[part, :], up[part, :], spread[start : start + tile, :]
                )
                for m, value in enumerate((gate_grad, up_grad, hidden)):
                    sums[m * R : (m + 1) * R, :] += jnp.dot(
                        proj_ff[m * R : (m + 1) * R, start : start + tile],
                        value,
                        preferred_element_type=jnp.float32,
                    )
                start += tile
        for m in range(2):
            for p in range(hid):
                own = sums[m * R + p * shares : m * R + (p + 1) * shares, :]
                ready[p, m * shares : (m + 1) * shares, :] = own
        member = membership(ids[...], examples)
        total_rows = member.shape[1]
        for j in range(shares):
            every = pl.ds(j, hid, shares)
            own = jnp.concatenate([flipped[k, every, :] for k in range(flipped.shape[0])], axis=1)
            left = (own[:, None, :] * member[None, :, :]).reshape(hid * examples, total_rows)
            product = exact_dot(left, sums[2 * R :, :], ((1,), (1,)))
            ready[:, 2 * shares :, j * R : (j + 1) * R] = product.reshape(hid, examples, R)


def backward(places, chips, blocks, weight, gates, ups, proj, proj_ff, ids, depth_tile, tile):
    rows = blocks[0].shape[0] * chips * 2
    width, depth = weight.shape
    hid = 2 * chips
    shares, examples = R // hid, rows // EX_TOK
    deep = 2 * shares + examples

    def stay(*shape):
        return pl.BlockSpec(shape, lambda k: (0,) * len(shape))

    return pl.pallas_call(
        functools.partial(backward_kernel, places, chips, examples, tile, len(gates)),
        grid=(depth // depth_tile,),
        out_shape=jax.ShapeDtypeStruct((hid, deep, rows), jnp.float32),
        in_specs=[pl.BlockSpec(memory_space=pl.ANY)] * len(blocks)
        + [
            pl.BlockSpec((width // SPLIT, depth_tile), lambda k, q=q: (q, k))
            for q in range(SPLIT)
        ]
        + [
            pl.BlockSpec((3 * R, depth_tile), lambda k: (0, k)),
            stay(3 * R, width),
            stay(1, rows),
        ]
        + [stay(*value.shape) for value in (*gates, *ups)],
        out_specs=stay(hid, deep, rows),
        scratch_shapes=[
            pltpu.VMEM((rows, depth), jnp.bfloat16),
            pltpu.VMEM((width, rows), jnp.float32),
            pltpu.VMEM((rows // 128, R, 128), jnp.float32),
            pltpu.VMEM((3 * R, rows), jnp.float32),
            pltpu.SemaphoreType.DMA((len(blocks),)),
        ],
        compiler_params=pltpu.CompilerParams(vmem_limit_bytes=32 * MEBI),
        cost_estimate=pl.CostEstimate(
            flops=2 * rows * depth * width, bytes_accessed=2 * depth * width, transcendentals=0
        ),
    )(*blocks, *[weight] * SPLIT, proj, proj_ff, ids, *gates, *ups)


def features_kernel(hid, received, inputs, ids, tests, features, partial):
    shares = R // hid
    examples = features.shape[0]
    member = membership(ids[...], examples)
    total = jnp.sum(received[...], axis=0)
    for m in range(2):
        own = total[m * shares : (m + 1) * shares]
        left = (own[:, None, :] * member[None, :, :]).reshape(shares * examples, own.shape[1])
        product = exact_dot(left, inputs[m * R : (m + 1) * R, :], ((1,), (1,)))
        for j in range(shares):
            start = (j * 3 + m) * R
            features[:, start : start + R] = product[j * examples : (j + 1) * examples]
    for j in range(shares):
        start = (j * 3 + 2) * R
        features[:, start : start + R] = total[2 * shares :, j * R : (j + 1) * R]
    scores = exact_dot(features[...], tests[...].astype(jnp.float32), ((1,), (1,)))
    partial[...] = jnp.broadcast_to(scores[None], partial.shape)


def finish(received, inputs, ids, tests):
    hid = received.shape[0]
    examples = ids.shape[1] // EX_TOK
    vmem = pl.BlockSpec(memory_space=pltpu.VMEM)
    return pl.pallas_call(
        functools.partial(features_kernel, hid),
        out_shape=(
            jax.ShapeDtypeStruct((examples, tests.shape[1]), jnp.float32),
            jax.ShapeDtypeStruct((hid, examples, tests.shape[0]), jnp.float32),
        ),
        in_specs=[vmem] * 4,
        out_specs=(vmem, vmem),
        compiler_params=pltpu.CompilerParams(vmem_limit_bytes=24 * MEBI),
    )(received, inputs, ids, tests)


def local_ring(
    tokens,
    out_grad,
    gate_weight,
    up_weight,
    down_weight,
    proj_d,
    proj_ff,
    example_ids,
    test_features,
):
    chips = lax.axis_size("hid") // 2
    ids = example_ids[None, :]
    places, token_blocks = gather_blocks(tokens, chips)
    _, grad_blocks = gather_blocks(out_grad, chips)
    gate, up = forward(places, chips, token_blocks, gate_weight, up_weight, TILE)
    send = backward(
        places, chips, grad_blocks, down_weight, [gate], [up], proj_d.T, proj_ff.T, ids, 1024, TILE
    )
    received = lax.all_to_all(send, "hid", 0, 0)
    inputs = project_inputs(places, chips, token_blocks, proj_d.T)
    features, partial = finish(received, inputs, ids, test_features)
    scores = jnp.sum(lax.all_to_all(partial, "hid", 0, 0), axis=0)
    return features, scores


def solution(mesh):
    one_ring = mesh.shape["mod"] == 1 and mesh.shape["hid"] <= 16
    return jax.shard_map(
        local_ring if one_ring else local_general,
        mesh=mesh,
        in_specs=(
            P(("groups", "hid"), "mod"),
            P(("groups", "hid"), "mod"),
            P("mod", "hid"),
            P("mod", "hid"),
            P("hid", "mod"),
            P("mod", None),
            P("hid", None),
            P("groups"),
            P("groups", "hid"),
        ),
        out_specs=(P("groups", "hid"), P("groups", None)),
        check_vma=False,
    )
```

```python
import functools

import jax
import jax.numpy as jnp
from jax import lax
from jax.experimental import pallas as pl
from jax.experimental.pallas import tpu as pltpu
from jax.sharding import PartitionSpec as P

R = 64
EX_TOK = 32
TILE = 256
PIECES = 4
DEPTH = 2048
SPLIT = 4
MEBI = 1024 * 1024
HIGH = lax.Precision.HIGHEST


def project_rows(block_rows, weights):
    return jnp.dot(block_rows, weights, preferred_element_type=jnp.float32)


def local_general(
    tokens,
    out_grad,
    gate_weight,
    up_weight,
    down_weight,
    proj_d,
    proj_ff,
    example_ids,
    test_features,
):
    width = gate_weight.shape[1]
    input_proj = proj_d[:, : 2 * R]
    output_proj = proj_d[:, 2 * R :]
    block_rows = lax.all_gather(tokens, "hid", axis=0, tiled=True)
    forward = jnp.concatenate(
        [
            project_rows(block_rows, gate_weight),
            project_rows(block_rows, up_weight),
            project_rows(block_rows, input_proj),
        ],
        axis=1,
    )
    block_rows = lax.all_gather(out_grad, "hid", axis=0, tiled=True)
    spread = lax.dot_general(
        block_rows, down_weight, (((1,), (1,)), ((), ())), preferred_element_type=jnp.float32
    )
    backward = jnp.concatenate([spread, project_rows(block_rows, output_proj)], axis=1)
    forward = lax.psum(forward, "mod")
    backward = lax.psum(backward, "mod")
    gate_act = forward[:, :width]
    up_act = forward[:, width : 2 * width]
    input_gate = forward[:, 2 * width : 2 * width + R]
    input_up = forward[:, 2 * width + R :]
    hidden_grad = backward[:, :width]
    output_down = backward[:, width:]
    hidden, gate_grad, up_grad = pointwise(gate_act, up_act, hidden_grad)
    output_gate = project_rows(gate_grad, proj_ff[:, :R])
    output_up = project_rows(up_grad, proj_ff[:, R : 2 * R])
    input_down = project_rows(hidden, proj_ff[:, 2 * R :])
    shares = R // lax.axis_size("hid")
    offset = lax.axis_index("hid") * shares
    output_gate, output_up, input_down = lax.psum((output_gate, output_up, input_down), "hid")
    own_gate = lax.dynamic_slice_in_dim(output_gate, offset, shares, 1)
    own_up = lax.dynamic_slice_in_dim(output_up, offset, shares, 1)
    own_down = lax.dynamic_slice_in_dim(output_down, offset, shares, 1)
    outputs = jnp.stack([own_gate, own_up, own_down], axis=2)
    inputs = jnp.stack([input_gate, input_up, input_down], axis=1)
    total_rows = outputs.shape[0]
    outer = (outputs[:, :, :, None] * inputs[:, None, :, :]).reshape(total_rows, shares * 3 * R)
    examples = example_ids.shape[0] // EX_TOK
    member = (example_ids[None, :] == jnp.arange(examples, dtype=jnp.int32)[:, None]).astype(
        jnp.float32
    )
    features = jnp.dot(member, outer, precision=HIGH, preferred_element_type=jnp.float32)
    partial_scores = jnp.dot(
        features,
        test_features.astype(jnp.float32).T,
        precision=HIGH,
        preferred_element_type=jnp.float32,
    )
    scores = lax.psum(partial_scores, "hid")
    return (features, scores)


def pointwise(gate_act, up_act, hidden_grad):
    sig = jax.nn.sigmoid(gate_act)
    hidden = (gate_act * sig * up_act).astype(jnp.bfloat16)
    gate_grad = (hidden_grad * up_act * sig * (1.0 + gate_act * (1.0 - sig))).astype(jnp.bfloat16)
    up_grad = (hidden_grad * gate_act * sig).astype(jnp.bfloat16)
    return hidden, gate_grad, up_grad


def ring_device(position, core, chips):
    height = chips // 2
    if isinstance(position, int):
        back = position >= height
        z = 2 * height - 1 - position if back else position
        return z * 4 + int(back) * 2 + core
    back = (position >= height).astype(jnp.int32)
    z = position + back * (2 * height - 1 - 2 * position)
    return z * 4 + back * 2 + core


def ring_position(device, chips):
    z, x = device // 4, (device // 2) % 2
    return z + x * (chips - 1 - 2 * z)


def ring_step(block, chips, step):
    pairs = [
        (ring_device(r, core, chips), ring_device((r + step) % chips, core, chips))
        for r in range(chips)
        for core in range(2)
    ]
    return lax.ppermute(block, "hid", pairs)


def core_swap(block, chips):
    return lax.ppermute(block, "hid", [(h, h ^ 1) for h in range(2 * chips)])


def gather_blocks(own, chips, last):
    places, blocks = [], []

    def found(offset, column, block):
        for other in range(2):
            places.append((offset, other, column))
            blocks.append(core_swap(block, chips) if other else block)

    found(0, 0, own)
    ahead, behind = own, own
    for step in range(1, chips // 2):
        ahead = ring_step(ahead, chips, 1)
        behind = ring_step(behind, chips, -1)
        found(-step, 0, ahead)
        found(step, 0, behind)
    across = chips // 2
    found(across, 0, ring_step(ahead if last > 0 else behind, chips, last))
    return places, blocks


def assemble(places, chips, blocks, whole, sems):
    device = lax.axis_index("hid")
    position, core = ring_position(device, chips), device % 2
    copies = []
    for index, (offset, other, column) in enumerate(places):
        rows, columns = blocks[index].shape
        source_core = core + other - 2 * core * other
        source = ring_device((position + offset + chips) % chips, source_core, chips)
        start = pl.multiple_of(source * rows, rows)
        target = whole.at[pl.ds(start, rows), pl.ds(column, columns)]
        copies.append(pltpu.make_async_copy(blocks[index], target, sems.at[index]))
    for copy in copies:
        copy.start()
    for copy in copies:
        copy.wait()


def last_dot(a, b):
    return lax.dot_general(a, b, (((1,), (1,)), ((), ())), preferred_element_type=jnp.float32)


def forward_kernel(places, chips, *refs):
    count = len(places)
    blocks, refs = refs[:count], refs[count:]
    gate_weight, up_weight, proj, gate, up, inputs, gate_sum, up_sum, whole, sems = refs
    n, k = pl.program_id(0), pl.program_id(1)

    @pl.when((n == 0) & (k == 0))
    def _():
        assemble(places, chips, blocks, whole, sems)
        inputs[...] = jnp.zeros_like(inputs)

    depth = gate_weight.shape[0]
    x = whole[:, pl.ds(pl.multiple_of(k * depth, depth), depth)]
    gate_part = jnp.dot(x, gate_weight[...], preferred_element_type=jnp.float32)
    up_part = jnp.dot(x, up_weight[...], preferred_element_type=jnp.float32)

    @pl.when(n < PIECES)
    def _():
        piece = depth // PIECES
        part = pl.ds(pl.multiple_of(k * depth + n * piece, piece), piece)
        inputs[...] += last_dot(proj[: 2 * R, part], whole[:, part])

    @pl.when(k == 0)
    def _():
        gate_sum[...] = gate_part
        up_sum[...] = up_part

    @pl.when(k == 1)
    def _():
        gate[...] = (gate_sum[...] + gate_part).T
        up[...] = (up_sum[...] + up_part).T


def forward(places, chips, blocks, gate_weight, up_weight, proj, tile):
    depth, width = gate_weight.shape
    rows = blocks[0].shape[0] * chips * 2
    return pl.pallas_call(
        functools.partial(forward_kernel, places, chips),
        grid=(width // tile, 2),
        out_shape=[jax.ShapeDtypeStruct((width, rows), jnp.float32)] * 2
        + [jax.ShapeDtypeStruct((2 * R, rows), jnp.float32)],
        in_specs=[pl.BlockSpec(memory_space=pl.ANY)] * len(blocks)
        + [pl.BlockSpec((depth // 2, tile), lambda n, k: (k, n))] * 2
        + [pl.BlockSpec((3 * R, depth), lambda n, k: (0, 0))],
        out_specs=[pl.BlockSpec((tile, rows), lambda n, k: (n, 0))] * 2
        + [pl.BlockSpec((2 * R, rows), lambda n, k: (0, 0))],
        scratch_shapes=[
            pltpu.VMEM((rows, tile), jnp.float32),
            pltpu.VMEM((rows, tile), jnp.float32),
            pltpu.VMEM((rows, depth), jnp.bfloat16),
            pltpu.SemaphoreType.DMA((len(blocks),)),
        ],
        compiler_params=pltpu.CompilerParams(vmem_limit_bytes=28 * MEBI),
        cost_estimate=pl.CostEstimate(
            flops=4 * rows * depth * width, bytes_accessed=4 * depth * width, transcendentals=0
        ),
    )(*blocks, gate_weight, up_weight, proj)


def membership(ids, examples):
    rows = lax.broadcasted_iota(jnp.int32, (examples, ids.shape[1]), 0)
    return (jnp.broadcast_to(ids, rows.shape) == rows).astype(jnp.float32)


def exact_dot(a, b, contract):
    return lax.dot_general(
        a, b, (contract, ((), ())), precision=HIGH, preferred_element_type=jnp.float32
    )


def backward_kernel(places, chips, examples, tile, parts, *refs):
    count = len(places)
    blocks, refs = refs[:count], refs[count:]
    weights, refs = refs[:SPLIT], refs[SPLIT:]
    proj, proj_ff, ids = refs[:3]
    gates, ups = refs[3 : 3 + parts], refs[3 + parts : 3 + 2 * parts]
    ready, whole, spread, flipped, sums, sems = refs[3 + 2 * parts :]
    step = pl.program_id(0)
    hid = 2 * chips
    shares = R // hid

    @pl.when(step == 0)
    def _():
        assemble(places, chips, blocks, whole, sems)
        spread[...] = jnp.zeros_like(spread)
        flipped[...] = jnp.zeros_like(flipped)

    height, depth = weights[0].shape
    x = whole[:, pl.ds(pl.multiple_of(step * depth, depth), depth)]
    for q, weight in enumerate(weights):
        spread[q * height : (q + 1) * height, :] += last_dot(weight[...], x)
    turned = last_dot(proj[2 * R :, :], x)
    for lanes in range(flipped.shape[0]):
        flipped[lanes] += turned[:, lanes * 128 : (lanes + 1) * 128]

    @pl.when(step == pl.num_programs(0) - 1)
    def _():
        sums[...] = jnp.zeros_like(sums)
        start = 0
        for gate, up in zip(gates, ups):
            for local in range(0, gate.shape[0], tile):
                part = pl.ds(local, tile)
                hidden, gate_grad, up_grad = pointwise(
                    gate[part, :], up[part, :], spread[start : start + tile, :]
                )
                for m, value in enumerate((gate_grad, up_grad, hidden)):
                    sums[m * R : (m + 1) * R, :] += jnp.dot(
                        proj_ff[m * R : (m + 1) * R, start : start + tile],
                        value,
                        preferred_element_type=jnp.float32,
                    )
                start += tile
        for m in range(2):
            for p in range(hid):
                own = sums[m * R + p * shares : m * R + (p + 1) * shares, :]
                ready[p, m * shares : (m + 1) * shares, :] = own
        member = membership(ids[...], examples)
        total_rows = member.shape[1]
        for j in range(shares):
            every = pl.ds(j, hid, shares)
            own = jnp.concatenate([flipped[k, every, :] for k in range(flipped.shape[0])], axis=1)
            left = (own[:, None, :] * member[None, :, :]).reshape(hid * examples, total_rows)
            product = exact_dot(left, sums[2 * R :, :], ((1,), (1,)))
            ready[:, 2 * shares :, j * R : (j + 1) * R] = product.reshape(hid, examples, R)


def backward(places, chips, blocks, weight, gates, ups, proj, proj_ff, ids, depth_tile, tile):
    rows = blocks[0].shape[0] * chips * 2
    width, depth = weight.shape
    hid = 2 * chips
    shares, examples = R // hid, rows // EX_TOK
    deep = 2 * shares + examples

    def stay(*shape):
        return pl.BlockSpec(shape, lambda k: (0,) * len(shape))

    return pl.pallas_call(
        functools.partial(backward_kernel, places, chips, examples, tile, len(gates)),
        grid=(depth // depth_tile,),
        out_shape=jax.ShapeDtypeStruct((hid, deep, rows), jnp.float32),
        in_specs=[pl.BlockSpec(memory_space=pl.ANY)] * len(blocks)
        + [
            pl.BlockSpec((width // SPLIT, depth_tile), lambda k, q=q: (q, k))
            for q in range(SPLIT)
        ]
        + [
            pl.BlockSpec((3 * R, depth_tile), lambda k: (0, k)),
            stay(3 * R, width),
            stay(1, rows),
        ]
        + [stay(*value.shape) for value in (*gates, *ups)],
        out_specs=stay(hid, deep, rows),
        scratch_shapes=[
            pltpu.VMEM((rows, depth), jnp.bfloat16),
            pltpu.VMEM((width, rows), jnp.float32),
            pltpu.VMEM((rows // 128, R, 128), jnp.float32),
            pltpu.VMEM((3 * R, rows), jnp.float32),
            pltpu.SemaphoreType.DMA((len(blocks),)),
        ],
        compiler_params=pltpu.CompilerParams(vmem_limit_bytes=32 * MEBI),
        cost_estimate=pl.CostEstimate(
            flops=2 * rows * depth * width, bytes_accessed=2 * depth * width, transcendentals=0
        ),
    )(*blocks, *[weight] * SPLIT, proj, proj_ff, ids, *gates, *ups)


def features_kernel(hid, received, inputs, ids, tests, features, partial):
    shares = R // hid
    examples = features.shape[0]
    member = membership(ids[...], examples)
    total = jnp.sum(received[...], axis=0)
    for m in range(2):
        own = total[m * shares : (m + 1) * shares]
        left = (own[:, None, :] * member[None, :, :]).reshape(shares * examples, own.shape[1])
        product = exact_dot(left, inputs[m * R : (m + 1) * R, :], ((1,), (1,)))
        for j in range(shares):
            start = (j * 3 + m) * R
            features[:, start : start + R] = product[j * examples : (j + 1) * examples]
    for j in range(shares):
        start = (j * 3 + 2) * R
        features[:, start : start + R] = total[2 * shares :, j * R : (j + 1) * R]
    scores = exact_dot(features[...], tests[...].astype(jnp.float32), ((1,), (1,)))
    partial[...] = jnp.broadcast_to(scores[None], partial.shape)


def finish(received, inputs, ids, tests):
    hid = received.shape[0]
    examples = ids.shape[1] // EX_TOK
    vmem = pl.BlockSpec(memory_space=pltpu.VMEM)
    return pl.pallas_call(
        functools.partial(features_kernel, hid),
        out_shape=(
            jax.ShapeDtypeStruct((examples, tests.shape[1]), jnp.float32),
            jax.ShapeDtypeStruct((hid, examples, tests.shape[0]), jnp.float32),
        ),
        in_specs=[vmem] * 4,
        out_specs=(vmem, vmem),
        compiler_params=pltpu.CompilerParams(vmem_limit_bytes=24 * MEBI),
    )(received, inputs, ids, tests)


def local_ring(
    tokens,
    out_grad,
    gate_weight,
    up_weight,
    down_weight,
    proj_d,
    proj_ff,
    example_ids,
    test_features,
):
    chips = lax.axis_size("hid") // 2
    ids = example_ids[None, :]
    places, token_blocks = gather_blocks(tokens, chips, 1)
    _, grad_blocks = gather_blocks(out_grad, chips, -1)
    gate, up, inputs = forward(
        places, chips, token_blocks, gate_weight, up_weight, proj_d.T, TILE
    )
    send = backward(
        places, chips, grad_blocks, down_weight, [gate], [up], proj_d.T, proj_ff.T, ids, 1024, TILE
    )
    received = lax.all_to_all(send, "hid", 0, 0)
    features, partial = finish(received, inputs, ids, test_features)
    scores = jnp.sum(lax.all_to_all(partial, "hid", 0, 0), axis=0)
    return features, scores


def solution(mesh):
    one_ring = mesh.shape["mod"] == 1 and mesh.shape["hid"] <= 16
    return jax.shard_map(
        local_ring if one_ring else local_general,
        mesh=mesh,
        in_specs=(
            P(("groups", "hid"), "mod"),
            P(("groups", "hid"), "mod"),
            P("mod", "hid"),
            P("mod", "hid"),
            P("hid", "mod"),
            P("mod", None),
            P("hid", None),
            P("groups"),
            P("groups", "hid"),
        ),
        out_specs=(P("groups", "hid"), P("groups", None)),
        check_vma=False,
    )
```

```python
import functools

import jax
import jax.numpy as jnp
from jax import lax
from jax.experimental import pallas as pl
from jax.experimental.pallas import tpu as pltpu
from jax.sharding import PartitionSpec as P

R = 64
EX_TOK = 32
TILE = 256
PIECES = 4
DEPTH = 2048
SPLIT = 4
MEBI = 1024 * 1024
HIGH = lax.Precision.HIGHEST


def project_rows(block_rows, weights):
    return jnp.dot(block_rows, weights, preferred_element_type=jnp.float32)


def local_general(
    tokens,
    out_grad,
    gate_weight,
    up_weight,
    down_weight,
    proj_d,
    proj_ff,
    example_ids,
    test_features,
):
    width = gate_weight.shape[1]
    input_proj = proj_d[:, : 2 * R]
    output_proj = proj_d[:, 2 * R :]
    block_rows = lax.all_gather(tokens, "hid", axis=0, tiled=True)
    forward = jnp.concatenate(
        [
            project_rows(block_rows, gate_weight),
            project_rows(block_rows, up_weight),
            project_rows(block_rows, input_proj),
        ],
        axis=1,
    )
    block_rows = lax.all_gather(out_grad, "hid", axis=0, tiled=True)
    spread = lax.dot_general(
        block_rows, down_weight, (((1,), (1,)), ((), ())), preferred_element_type=jnp.float32
    )
    backward = jnp.concatenate([spread, project_rows(block_rows, output_proj)], axis=1)
    forward = lax.psum(forward, "mod")
    backward = lax.psum(backward, "mod")
    gate_act = forward[:, :width]
    up_act = forward[:, width : 2 * width]
    input_gate = forward[:, 2 * width : 2 * width + R]
    input_up = forward[:, 2 * width + R :]
    hidden_grad = backward[:, :width]
    output_down = backward[:, width:]
    hidden, gate_grad, up_grad = pointwise(gate_act, up_act, hidden_grad)
    output_gate = project_rows(gate_grad, proj_ff[:, :R])
    output_up = project_rows(up_grad, proj_ff[:, R : 2 * R])
    input_down = project_rows(hidden, proj_ff[:, 2 * R :])
    shares = R // lax.axis_size("hid")
    offset = lax.axis_index("hid") * shares
    output_gate, output_up, input_down = lax.psum((output_gate, output_up, input_down), "hid")
    own_gate = lax.dynamic_slice_in_dim(output_gate, offset, shares, 1)
    own_up = lax.dynamic_slice_in_dim(output_up, offset, shares, 1)
    own_down = lax.dynamic_slice_in_dim(output_down, offset, shares, 1)
    outputs = jnp.stack([own_gate, own_up, own_down], axis=2)
    inputs = jnp.stack([input_gate, input_up, input_down], axis=1)
    total_rows = outputs.shape[0]
    outer = (outputs[:, :, :, None] * inputs[:, None, :, :]).reshape(total_rows, shares * 3 * R)
    examples = example_ids.shape[0] // EX_TOK
    member = (example_ids[None, :] == jnp.arange(examples, dtype=jnp.int32)[:, None]).astype(
        jnp.float32
    )
    features = jnp.dot(member, outer, precision=HIGH, preferred_element_type=jnp.float32)
    partial_scores = jnp.dot(
        features,
        test_features.astype(jnp.float32).T,
        precision=HIGH,
        preferred_element_type=jnp.float32,
    )
    scores = lax.psum(partial_scores, "hid")
    return (features, scores)


def pointwise(gate_act, up_act, hidden_grad):
    sig = jax.nn.sigmoid(gate_act)
    hidden = (gate_act * sig * up_act).astype(jnp.bfloat16)
    gate_grad = (hidden_grad * up_act * sig * (1.0 + gate_act * (1.0 - sig))).astype(jnp.bfloat16)
    up_grad = (hidden_grad * gate_act * sig).astype(jnp.bfloat16)
    return hidden, gate_grad, up_grad


def ring_device(position, core, chips):
    height = chips // 2
    if isinstance(position, int):
        back = position >= height
        z = 2 * height - 1 - position if back else position
        return z * 4 + int(back) * 2 + core
    back = (position >= height).astype(jnp.int32)
    z = position + back * (2 * height - 1 - 2 * position)
    return z * 4 + back * 2 + core


def ring_position(device, chips):
    z, x = device // 4, (device // 2) % 2
    return z + x * (chips - 1 - 2 * z)


def ring_step(block, chips, step):
    pairs = [
        (ring_device(r, core, chips), ring_device((r + step) % chips, core, chips))
        for r in range(chips)
        for core in range(2)
    ]
    return lax.ppermute(block, "hid", pairs)


def core_swap(block, chips):
    return lax.ppermute(block, "hid", [(h, h ^ 1) for h in range(2 * chips)])


def gather_blocks(own, chips, last):
    offsets, blocks = [0], [own]
    ahead, behind = own, own
    for step in range(1, chips // 2):
        ahead = ring_step(ahead, chips, 1)
        behind = ring_step(behind, chips, -1)
        offsets += [-step, step]
        blocks += [ahead, behind]
    offsets.append(chips // 2)
    blocks.append(ring_step(ahead if last > 0 else behind, chips, last))
    return [(offset, other, 0) for other in range(2) for offset in offsets], blocks


def after(value, other):
    return lax.optimization_barrier((value, other))[0]


def assemble(places, chips, blocks, whole, sems):
    device = lax.axis_index("hid")
    position, core = ring_position(device, chips), device % 2
    copies = []
    for index, (offset, other, column) in enumerate(places):
        rows, columns = blocks[index].shape
        source_core = core + other - 2 * core * other
        source = ring_device((position + offset + chips) % chips, source_core, chips)
        start = pl.multiple_of(source * rows, rows)
        target = whole.at[pl.ds(start, rows), pl.ds(column, columns)]
        copies.append(pltpu.make_async_copy(blocks[index], target, sems.at[index]))
    for copy in copies:
        copy.start()
    for copy in copies:
        copy.wait()


def last_dot(a, b):
    return lax.dot_general(a, b, (((1,), (1,)), ((), ())), preferred_element_type=jnp.float32)


def forward_kernel(places, chips, *refs):
    count = len(places)
    blocks, refs = refs[:count], refs[count:]
    gate_weight, up_weight, proj, gate, up, inputs, gate_sum, up_sum, whole, sems = refs
    n, k = pl.program_id(0), pl.program_id(1)

    @pl.when((n == 0) & (k == 0))
    def _():
        assemble(places, chips, blocks, whole, sems)
        inputs[...] = jnp.zeros_like(inputs)

    depth = gate_weight.shape[0]
    x = whole[:, pl.ds(pl.multiple_of(k * depth, depth), depth)]
    gate_part = jnp.dot(x, gate_weight[...], preferred_element_type=jnp.float32)
    up_part = jnp.dot(x, up_weight[...], preferred_element_type=jnp.float32)

    @pl.when(n < PIECES)
    def _():
        piece = depth // PIECES
        part = pl.ds(pl.multiple_of(k * depth + n * piece, piece), piece)
        inputs[...] += last_dot(proj[: 2 * R, part], whole[:, part])

    @pl.when(k == 0)
    def _():
        gate_sum[...] = gate_part
        up_sum[...] = up_part

    @pl.when(k == 1)
    def _():
        gate[...] = (gate_sum[...] + gate_part).T
        up[...] = (up_sum[...] + up_part).T


def forward(places, chips, blocks, gate_weight, up_weight, proj, tile):
    depth, width = gate_weight.shape
    rows = blocks[0].shape[0] * chips * 2
    return pl.pallas_call(
        functools.partial(forward_kernel, places, chips),
        grid=(width // tile, 2),
        out_shape=[jax.ShapeDtypeStruct((width, rows), jnp.float32)] * 2
        + [jax.ShapeDtypeStruct((2 * R, rows), jnp.float32)],
        in_specs=[pl.BlockSpec(memory_space=pl.ANY)] * len(blocks)
        + [pl.BlockSpec((depth // 2, tile), lambda n, k: (k, n))] * 2
        + [pl.BlockSpec((3 * R, depth), lambda n, k: (0, 0))],
        out_specs=[pl.BlockSpec((tile, rows), lambda n, k: (n, 0))] * 2
        + [pl.BlockSpec((2 * R, rows), lambda n, k: (0, 0))],
        scratch_shapes=[
            pltpu.VMEM((rows, tile), jnp.float32),
            pltpu.VMEM((rows, tile), jnp.float32),
            pltpu.VMEM((rows, depth), jnp.bfloat16),
            pltpu.SemaphoreType.DMA((len(blocks),)),
        ],
        compiler_params=pltpu.CompilerParams(vmem_limit_bytes=28 * MEBI),
        cost_estimate=pl.CostEstimate(
            flops=4 * rows * depth * width, bytes_accessed=4 * depth * width, transcendentals=0
        ),
    )(*blocks, gate_weight, up_weight, proj)


def membership(ids, examples):
    rows = lax.broadcasted_iota(jnp.int32, (examples, ids.shape[1]), 0)
    return (jnp.broadcast_to(ids, rows.shape) == rows).astype(jnp.float32)


def exact_dot(a, b, contract):
    return lax.dot_general(
        a, b, (contract, ((), ())), precision=HIGH, preferred_element_type=jnp.float32
    )


def backward_kernel(places, chips, examples, tile, parts, *refs):
    count = len(places)
    blocks, refs = refs[:count], refs[count:]
    weights, refs = refs[:SPLIT], refs[SPLIT:]
    proj, proj_ff, ids = refs[:3]
    gates, ups = refs[3 : 3 + parts], refs[3 + parts : 3 + 2 * parts]
    ready, whole, spread, flipped, sums, sems = refs[3 + 2 * parts :]
    step = pl.program_id(0)
    hid = 2 * chips
    shares = R // hid

    @pl.when(step == 0)
    def _():
        assemble(places, chips, blocks, whole, sems)
        spread[...] = jnp.zeros_like(spread)
        flipped[...] = jnp.zeros_like(flipped)

    height, depth = weights[0].shape
    x = whole[:, pl.ds(pl.multiple_of(step * depth, depth), depth)]
    for q, weight in enumerate(weights):
        spread[q * height : (q + 1) * height, :] += last_dot(weight[...], x)
    turned = last_dot(proj[2 * R :, :], x)
    for lanes in range(flipped.shape[0]):
        flipped[lanes] += turned[:, lanes * 128 : (lanes + 1) * 128]

    @pl.when(step == pl.num_programs(0) - 1)
    def _():
        sums[...] = jnp.zeros_like(sums)
        start = 0
        for gate, up in zip(gates, ups):
            for local in range(0, gate.shape[0], tile):
                part = pl.ds(local, tile)
                hidden, gate_grad, up_grad = pointwise(
                    gate[part, :], up[part, :], spread[start : start + tile, :]
                )
                for m, value in enumerate((gate_grad, up_grad, hidden)):
                    sums[m * R : (m + 1) * R, :] += jnp.dot(
                        proj_ff[m * R : (m + 1) * R, start : start + tile],
                        value,
                        preferred_element_type=jnp.float32,
                    )
                start += tile
        for m in range(2):
            for p in range(hid):
                own = sums[m * R + p * shares : m * R + (p + 1) * shares, :]
                ready[p, m * shares : (m + 1) * shares, :] = own
        member = membership(ids[...], examples)
        total_rows = member.shape[1]
        for j in range(shares):
            every = pl.ds(j, hid, shares)
            own = jnp.concatenate([flipped[k, every, :] for k in range(flipped.shape[0])], axis=1)
            left = (own[:, None, :] * member[None, :, :]).reshape(hid * examples, total_rows)
            product = exact_dot(left, sums[2 * R :, :], ((1,), (1,)))
            ready[:, 2 * shares :, j * R : (j + 1) * R] = product.reshape(hid, examples, R)


def backward(places, chips, blocks, weight, gates, ups, proj, proj_ff, ids, depth_tile, tile):
    rows = blocks[0].shape[0] * chips * 2
    width, depth = weight.shape
    hid = 2 * chips
    shares, examples = R // hid, rows // EX_TOK
    deep = 2 * shares + examples

    def stay(*shape):
        return pl.BlockSpec(shape, lambda k: (0,) * len(shape))

    return pl.pallas_call(
        functools.partial(backward_kernel, places, chips, examples, tile, len(gates)),
        grid=(depth // depth_tile,),
        out_shape=jax.ShapeDtypeStruct((hid, deep, rows), jnp.float32),
        in_specs=[pl.BlockSpec(memory_space=pl.ANY)] * len(blocks)
        + [
            pl.BlockSpec((width // SPLIT, depth_tile), lambda k, q=q: (q, k))
            for q in range(SPLIT)
        ]
        + [
            pl.BlockSpec((3 * R, depth_tile), lambda k: (0, k)),
            stay(3 * R, width),
            stay(1, rows),
        ]
        + [stay(*value.shape) for value in (*gates, *ups)],
        out_specs=stay(hid, deep, rows),
        scratch_shapes=[
            pltpu.VMEM((rows, depth), jnp.bfloat16),
            pltpu.VMEM((width, rows), jnp.float32),
            pltpu.VMEM((rows // 128, R, 128), jnp.float32),
            pltpu.VMEM((3 * R, rows), jnp.float32),
            pltpu.SemaphoreType.DMA((len(blocks),)),
        ],
        compiler_params=pltpu.CompilerParams(vmem_limit_bytes=32 * MEBI),
        cost_estimate=pl.CostEstimate(
            flops=2 * rows * depth * width, bytes_accessed=2 * depth * width, transcendentals=0
        ),
    )(*blocks, *[weight] * SPLIT, proj, proj_ff, ids, *gates, *ups)


def features_kernel(hid, received, inputs, ids, tests, features, partial):
    shares = R // hid
    examples = features.shape[0]
    member = membership(ids[...], examples)
    total = jnp.sum(received[...], axis=0)
    for m in range(2):
        own = total[m * shares : (m + 1) * shares]
        left = (own[:, None, :] * member[None, :, :]).reshape(shares * examples, own.shape[1])
        product = exact_dot(left, inputs[m * R : (m + 1) * R, :], ((1,), (1,)))
        for j in range(shares):
            start = (j * 3 + m) * R
            features[:, start : start + R] = product[j * examples : (j + 1) * examples]
    for j in range(shares):
        start = (j * 3 + 2) * R
        features[:, start : start + R] = total[2 * shares :, j * R : (j + 1) * R]
    scores = exact_dot(features[...], tests[...].astype(jnp.float32), ((1,), (1,)))
    partial[...] = jnp.broadcast_to(scores[None], partial.shape)


def finish(received, inputs, ids, tests):
    hid = received.shape[0]
    examples = ids.shape[1] // EX_TOK
    vmem = pl.BlockSpec(memory_space=pltpu.VMEM)
    return pl.pallas_call(
        functools.partial(features_kernel, hid),
        out_shape=(
            jax.ShapeDtypeStruct((examples, tests.shape[1]), jnp.float32),
            jax.ShapeDtypeStruct((hid, examples, tests.shape[0]), jnp.float32),
        ),
        in_specs=[vmem] * 4,
        out_specs=(vmem, vmem),
        compiler_params=pltpu.CompilerParams(vmem_limit_bytes=24 * MEBI),
    )(received, inputs, ids, tests)


def local_ring(
    tokens,
    out_grad,
    gate_weight,
    up_weight,
    down_weight,
    proj_d,
    proj_ff,
    example_ids,
    test_features,
):
    chips = lax.axis_size("hid") // 2
    ids = example_ids[None, :]
    places, token_blocks = gather_blocks(tokens, chips, 1)
    _, grad_blocks = gather_blocks(out_grad, chips, -1)
    token_blocks = token_blocks + [core_swap(block, chips) for block in token_blocks]
    token_blocks[0] = after(token_blocks[0], grad_blocks[-2])
    gate, up, inputs = forward(
        places, chips, token_blocks, gate_weight, up_weight, proj_d.T, TILE
    )
    early = [core_swap(block, chips) for block in grad_blocks[:-3]]
    late = [core_swap(after(block, gate), chips) for block in grad_blocks[-3:]]
    grad_blocks = grad_blocks + early + late
    send = backward(
        places, chips, grad_blocks, down_weight, [gate], [up], proj_d.T, proj_ff.T, ids, 1024, TILE
    )
    received = lax.all_to_all(send, "hid", 0, 0)
    features, partial = finish(received, inputs, ids, test_features)
    scores = jnp.sum(lax.all_to_all(partial, "hid", 0, 0), axis=0)
    return features, scores


def solution(mesh):
    one_ring = mesh.shape["mod"] == 1 and mesh.shape["hid"] <= 16
    return jax.shard_map(
        local_ring if one_ring else local_general,
        mesh=mesh,
        in_specs=(
            P(("groups", "hid"), "mod"),
            P(("groups", "hid"), "mod"),
            P("mod", "hid"),
            P("mod", "hid"),
            P("hid", "mod"),
            P("mod", None),
            P("hid", None),
            P("groups"),
            P("groups", "hid"),
        ),
        out_specs=(P("groups", "hid"), P("groups", None)),
        check_vma=False,
    )
```

```python
import functools

import jax
import jax.numpy as jnp
from jax import lax
from jax.experimental import pallas as pl
from jax.experimental.pallas import tpu as pltpu
from jax.sharding import PartitionSpec as P

R = 64
EX_TOK = 32
TILE = 256
PIECES = 4
DEPTH = 2048
SPLIT = 4
MEBI = 1024 * 1024
HIGH = lax.Precision.HIGHEST


def project_rows(block_rows, weights):
    return jnp.dot(block_rows, weights, preferred_element_type=jnp.float32)


def local_general(
    tokens,
    out_grad,
    gate_weight,
    up_weight,
    down_weight,
    proj_d,
    proj_ff,
    example_ids,
    test_features,
):
    width = gate_weight.shape[1]
    input_proj = proj_d[:, : 2 * R]
    output_proj = proj_d[:, 2 * R :]
    block_rows = lax.all_gather(tokens, "hid", axis=0, tiled=True)
    forward = jnp.concatenate(
        [
            project_rows(block_rows, gate_weight),
            project_rows(block_rows, up_weight),
            project_rows(block_rows, input_proj),
        ],
        axis=1,
    )
    block_rows = lax.all_gather(out_grad, "hid", axis=0, tiled=True)
    spread = lax.dot_general(
        block_rows, down_weight, (((1,), (1,)), ((), ())), preferred_element_type=jnp.float32
    )
    backward = jnp.concatenate([spread, project_rows(block_rows, output_proj)], axis=1)
    forward = lax.psum(forward, "mod")
    backward = lax.psum(backward, "mod")
    gate_act = forward[:, :width]
    up_act = forward[:, width : 2 * width]
    input_gate = forward[:, 2 * width : 2 * width + R]
    input_up = forward[:, 2 * width + R :]
    hidden_grad = backward[:, :width]
    output_down = backward[:, width:]
    hidden, gate_grad, up_grad = pointwise(gate_act, up_act, hidden_grad)
    output_gate = project_rows(gate_grad, proj_ff[:, :R])
    output_up = project_rows(up_grad, proj_ff[:, R : 2 * R])
    input_down = project_rows(hidden, proj_ff[:, 2 * R :])
    shares = R // lax.axis_size("hid")
    offset = lax.axis_index("hid") * shares
    output_gate, output_up, input_down = lax.psum((output_gate, output_up, input_down), "hid")
    own_gate = lax.dynamic_slice_in_dim(output_gate, offset, shares, 1)
    own_up = lax.dynamic_slice_in_dim(output_up, offset, shares, 1)
    own_down = lax.dynamic_slice_in_dim(output_down, offset, shares, 1)
    outputs = jnp.stack([own_gate, own_up, own_down], axis=2)
    inputs = jnp.stack([input_gate, input_up, input_down], axis=1)
    total_rows = outputs.shape[0]
    outer = (outputs[:, :, :, None] * inputs[:, None, :, :]).reshape(total_rows, shares * 3 * R)
    examples = example_ids.shape[0] // EX_TOK
    member = (example_ids[None, :] == jnp.arange(examples, dtype=jnp.int32)[:, None]).astype(
        jnp.float32
    )
    features = jnp.dot(member, outer, precision=HIGH, preferred_element_type=jnp.float32)
    partial_scores = jnp.dot(
        features,
        test_features.astype(jnp.float32).T,
        precision=HIGH,
        preferred_element_type=jnp.float32,
    )
    scores = lax.psum(partial_scores, "hid")
    return (features, scores)


def pointwise(gate_act, up_act, hidden_grad):
    sig = jax.nn.sigmoid(gate_act)
    hidden = (gate_act * sig * up_act).astype(jnp.bfloat16)
    gate_grad = (hidden_grad * up_act * sig * (1.0 + gate_act * (1.0 - sig))).astype(jnp.bfloat16)
    up_grad = (hidden_grad * gate_act * sig).astype(jnp.bfloat16)
    return hidden, gate_grad, up_grad


def ring_device(position, core, chips):
    height = chips // 2
    if isinstance(position, int):
        back = position >= height
        z = 2 * height - 1 - position if back else position
        return z * 4 + int(back) * 2 + core
    back = (position >= height).astype(jnp.int32)
    z = position + back * (2 * height - 1 - 2 * position)
    return z * 4 + back * 2 + core


def ring_position(device, chips):
    z, x = device // 4, (device // 2) % 2
    return z + x * (chips - 1 - 2 * z)


def ring_step(block, chips, step):
    pairs = [
        (ring_device(r, core, chips), ring_device((r + step) % chips, core, chips))
        for r in range(chips)
        for core in range(2)
    ]
    return lax.ppermute(block, "hid", pairs)


def core_swap(block, chips):
    return lax.ppermute(block, "hid", [(h, h ^ 1) for h in range(2 * chips)])


def gather_blocks(own, chips, last):
    offsets, blocks = [0], [own]
    ahead, behind = own, own
    for step in range(1, chips // 2):
        ahead = ring_step(ahead, chips, 1)
        behind = ring_step(behind, chips, -1)
        offsets += [-step, step]
        blocks += [ahead, behind]
    offsets.append(chips // 2)
    blocks.append(ring_step(ahead if last > 0 else behind, chips, last))
    return [(offset, other, 0) for other in range(2) for offset in offsets], blocks


def after(value, other):
    return lax.optimization_barrier((value, other))[0]


def assemble(places, chips, blocks, whole, sems):
    device = lax.axis_index("hid")
    position, core = ring_position(device, chips), device % 2
    copies = []
    for index, (offset, other, column) in enumerate(places):
        rows, columns = blocks[index].shape
        source_core = core + other - 2 * core * other
        source = ring_device((position + offset + chips) % chips, source_core, chips)
        start = pl.multiple_of(source * rows, rows)
        target = whole.at[pl.ds(start, rows), pl.ds(column, columns)]
        copies.append(pltpu.make_async_copy(blocks[index], target, sems.at[index]))
    for copy in copies:
        copy.start()
    for copy in copies:
        copy.wait()


def last_dot(a, b):
    return lax.dot_general(a, b, (((1,), (1,)), ((), ())), preferred_element_type=jnp.float32)


def forward_kernel(places, chips, *refs):
    count = len(places)
    blocks, refs = refs[:count], refs[count:]
    gate_weight, up_weight, proj, gate, up, inputs, gate_sum, up_sum, whole, sems = refs
    n, k = pl.program_id(0), pl.program_id(1)

    @pl.when((n == 0) & (k == 0))
    def _():
        assemble(places, chips, blocks, whole, sems)
        inputs[...] = jnp.zeros_like(inputs)

    depth = gate_weight.shape[0]
    x = whole[:, pl.ds(pl.multiple_of(k * depth, depth), depth)]
    gate_part = jnp.dot(x, gate_weight[...], preferred_element_type=jnp.float32)
    up_part = jnp.dot(x, up_weight[...], preferred_element_type=jnp.float32)

    @pl.when(n < PIECES)
    def _():
        piece = depth // PIECES
        part = pl.ds(pl.multiple_of(k * depth + n * piece, piece), piece)
        inputs[...] += last_dot(proj[: 2 * R, :], whole[:, part])

    @pl.when(k == 0)
    def _():
        gate_sum[...] = gate_part
        up_sum[...] = up_part

    @pl.when(k == 1)
    def _():
        gate[...] = (gate_sum[...] + gate_part).T
        up[...] = (up_sum[...] + up_part).T


def forward(places, chips, blocks, gate_weight, up_weight, proj, tile):
    depth, width = gate_weight.shape
    rows = blocks[0].shape[0] * chips * 2
    return pl.pallas_call(
        functools.partial(forward_kernel, places, chips),
        grid=(width // tile, 2),
        out_shape=[jax.ShapeDtypeStruct((width, rows), jnp.float32)] * 2
        + [jax.ShapeDtypeStruct((2 * R, rows), jnp.float32)],
        in_specs=[pl.BlockSpec(memory_space=pl.ANY)] * len(blocks)
        + [pl.BlockSpec((depth // 2, tile), lambda n, k: (k, n))] * 2
        + [
            pl.BlockSpec(
                (3 * R, depth // (2 * PIECES)),
                lambda n, k: (0, k * PIECES + jnp.minimum(n, PIECES - 1)),
            )
        ],
        out_specs=[pl.BlockSpec((tile, rows), lambda n, k: (n, 0))] * 2
        + [pl.BlockSpec((2 * R, rows), lambda n, k: (0, 0))],
        scratch_shapes=[
            pltpu.VMEM((rows, tile), jnp.float32),
            pltpu.VMEM((rows, tile), jnp.float32),
            pltpu.VMEM((rows, depth), jnp.bfloat16),
            pltpu.SemaphoreType.DMA((len(blocks),)),
        ],
        compiler_params=pltpu.CompilerParams(vmem_limit_bytes=28 * MEBI),
        cost_estimate=pl.CostEstimate(
            flops=4 * rows * depth * width, bytes_accessed=4 * depth * width, transcendentals=0
        ),
    )(*blocks, gate_weight, up_weight, proj)


def membership(ids, examples):
    rows = lax.broadcasted_iota(jnp.int32, (examples, ids.shape[1]), 0)
    return (jnp.broadcast_to(ids, rows.shape) == rows).astype(jnp.float32)


def exact_dot(a, b, contract):
    return lax.dot_general(
        a, b, (contract, ((), ())), precision=HIGH, preferred_element_type=jnp.float32
    )


def backward_kernel(places, chips, examples, tile, *refs):
    count = len(places)
    blocks, refs = refs[:count], refs[count:]
    weights, refs = refs[:SPLIT], refs[SPLIT:]
    proj, proj_ff, ids = refs[:3]
    gate_up, (ready, whole, spread, flipped, sums, gate, up, sems, late) = refs[3:5], refs[5:]
    fetches = [
        pltpu.make_async_copy(source, target, late.at[index])
        for index, (source, target) in enumerate(zip(gate_up, (gate, up)))
    ]
    step = pl.program_id(0)
    hid = 2 * chips
    shares = R // hid

    @pl.when(step == 0)
    def _():
        assemble(places, chips, blocks, whole, sems)
        for fetch in fetches:
            fetch.start()
        spread[...] = jnp.zeros_like(spread)
        flipped[...] = jnp.zeros_like(flipped)

    height, depth = weights[0].shape
    x = whole[:, pl.ds(pl.multiple_of(step * depth, depth), depth)]
    for q, weight in enumerate(weights):
        spread[q * height : (q + 1) * height, :] += last_dot(weight[...], x)
    turned = last_dot(proj[2 * R :, :], x)
    for lanes in range(flipped.shape[0]):
        flipped[lanes] += turned[:, lanes * 128 : (lanes + 1) * 128]

    @pl.when(step == pl.num_programs(0) - 1)
    def _():
        sums[...] = jnp.zeros_like(sums)
        for fetch in fetches:
            fetch.wait()
        for start in range(0, gate.shape[0], tile):
            part = pl.ds(start, tile)
            hidden, gate_grad, up_grad = pointwise(gate[part, :], up[part, :], spread[part, :])
            for m, value in enumerate((gate_grad, up_grad, hidden)):
                sums[m * R : (m + 1) * R, :] += jnp.dot(
                    proj_ff[m * R : (m + 1) * R, start : start + tile],
                    value,
                    preferred_element_type=jnp.float32,
                )
        for m in range(2):
            for p in range(hid):
                own = sums[m * R + p * shares : m * R + (p + 1) * shares, :]
                ready[p, m * shares : (m + 1) * shares, :] = own
        member = membership(ids[...], examples)
        total_rows = member.shape[1]
        for j in range(shares):
            every = pl.ds(j, hid, shares)
            own = jnp.concatenate([flipped[k, every, :] for k in range(flipped.shape[0])], axis=1)
            left = (own[:, None, :] * member[None, :, :]).reshape(hid * examples, total_rows)
            product = exact_dot(left, sums[2 * R :, :], ((1,), (1,)))
            ready[:, 2 * shares :, j * R : (j + 1) * R] = product.reshape(hid, examples, R)


def backward(places, chips, blocks, weight, gate, up, proj, proj_ff, ids, depth_tile, tile):
    rows = blocks[0].shape[0] * chips * 2
    width, depth = weight.shape
    hid = 2 * chips
    shares, examples = R // hid, rows // EX_TOK
    deep = 2 * shares + examples

    def stay(*shape):
        return pl.BlockSpec(shape, lambda k: (0,) * len(shape))

    return pl.pallas_call(
        functools.partial(backward_kernel, places, chips, examples, tile),
        grid=(depth // depth_tile,),
        out_shape=jax.ShapeDtypeStruct((hid, deep, rows), jnp.float32),
        in_specs=[pl.BlockSpec(memory_space=pl.ANY)] * len(blocks)
        + [
            pl.BlockSpec((width // SPLIT, depth_tile), lambda k, q=q: (q, k))
            for q in range(SPLIT)
        ]
        + [
            pl.BlockSpec((3 * R, depth_tile), lambda k: (0, k)),
            stay(3 * R, width),
            stay(1, rows),
        ]
        + [pl.BlockSpec(memory_space=pl.ANY)] * 2,
        out_specs=stay(hid, deep, rows),
        scratch_shapes=[
            pltpu.VMEM((rows, depth), jnp.bfloat16),
            pltpu.VMEM((width, rows), jnp.float32),
            pltpu.VMEM((rows // 128, R, 128), jnp.float32),
            pltpu.VMEM((3 * R, rows), jnp.float32),
            pltpu.VMEM((width, rows), jnp.float32),
            pltpu.VMEM((width, rows), jnp.float32),
            pltpu.SemaphoreType.DMA((len(blocks),)),
            pltpu.SemaphoreType.DMA((2,)),
        ],
        compiler_params=pltpu.CompilerParams(vmem_limit_bytes=32 * MEBI),
        cost_estimate=pl.CostEstimate(
            flops=2 * rows * depth * width, bytes_accessed=2 * depth * width, transcendentals=0
        ),
    )(*blocks, *[weight] * SPLIT, proj, proj_ff, ids, gate, up)


def features_kernel(hid, received, inputs, ids, tests, features, partial):
    shares = R // hid
    examples = features.shape[0]
    member = membership(ids[...], examples)
    total = jnp.sum(received[...], axis=0)
    for m in range(2):
        own = total[m * shares : (m + 1) * shares]
        left = (own[:, None, :] * member[None, :, :]).reshape(shares * examples, own.shape[1])
        product = exact_dot(left, inputs[m * R : (m + 1) * R, :], ((1,), (1,)))
        for j in range(shares):
            start = (j * 3 + m) * R
            features[:, start : start + R] = product[j * examples : (j + 1) * examples]
    for j in range(shares):
        start = (j * 3 + 2) * R
        features[:, start : start + R] = total[2 * shares :, j * R : (j + 1) * R]
    scores = exact_dot(features[...], tests[...].astype(jnp.float32), ((1,), (1,)))
    partial[...] = jnp.broadcast_to(scores[None], partial.shape)


def finish(received, inputs, ids, tests):
    hid = received.shape[0]
    examples = ids.shape[1] // EX_TOK
    vmem = pl.BlockSpec(memory_space=pltpu.VMEM)
    return pl.pallas_call(
        functools.partial(features_kernel, hid),
        out_shape=(
            jax.ShapeDtypeStruct((examples, tests.shape[1]), jnp.float32),
            jax.ShapeDtypeStruct((hid, examples, tests.shape[0]), jnp.float32),
        ),
        in_specs=[vmem] * 4,
        out_specs=(vmem, vmem),
        compiler_params=pltpu.CompilerParams(vmem_limit_bytes=24 * MEBI),
    )(received, inputs, ids, tests)


def local_ring(
    tokens,
    out_grad,
    gate_weight,
    up_weight,
    down_weight,
    proj_d,
    proj_ff,
    example_ids,
    test_features,
):
    chips = lax.axis_size("hid") // 2
    ids = example_ids[None, :]
    places, token_blocks = gather_blocks(tokens, chips, 1)
    _, grad_blocks = gather_blocks(out_grad, chips, -1)
    token_blocks = token_blocks + [core_swap(block, chips) for block in token_blocks]
    token_blocks[0] = after(token_blocks[0], grad_blocks[-2])
    gate, up, inputs = forward(
        places, chips, token_blocks, gate_weight, up_weight, proj_d.T, TILE
    )
    early = [core_swap(block, chips) for block in grad_blocks[:-3]]
    late = [core_swap(after(block, gate), chips) for block in grad_blocks[-3:]]
    grad_blocks = grad_blocks + early + late
    send = backward(
        places, chips, grad_blocks, down_weight, gate, up, proj_d.T, proj_ff.T, ids, 1024, TILE
    )
    received = lax.all_to_all(send, "hid", 0, 0)
    features, partial = finish(received, inputs, ids, test_features)
    scores = jnp.sum(lax.all_to_all(partial, "hid", 0, 0), axis=0)
    return features, scores


def solution(mesh):
    one_ring = mesh.shape["mod"] == 1 and mesh.shape["hid"] <= 16
    return jax.shard_map(
        local_ring if one_ring else local_general,
        mesh=mesh,
        in_specs=(
            P(("groups", "hid"), "mod"),
            P(("groups", "hid"), "mod"),
            P("mod", "hid"),
            P("mod", "hid"),
            P("hid", "mod"),
            P("mod", None),
            P("hid", None),
            P("groups"),
            P("groups", "hid"),
        ),
        out_specs=(P("groups", "hid"), P("groups", None)),
        check_vma=False,
    )
```

```python
import functools

import jax
import jax.numpy as jnp
from jax import lax
from jax.experimental import pallas as pl
from jax.experimental.pallas import tpu as pltpu
from jax.sharding import PartitionSpec as P

R = 64
EX_TOK = 32
TILE = 256
PIECES = 4
DEPTH = 2048
SPLIT = 4
MEBI = 1024 * 1024
HIGH = lax.Precision.HIGHEST


def project_rows(block_rows, weights):
    return jnp.dot(block_rows, weights, preferred_element_type=jnp.float32)


def local_general(
    tokens,
    out_grad,
    gate_weight,
    up_weight,
    down_weight,
    proj_d,
    proj_ff,
    example_ids,
    test_features,
):
    width = gate_weight.shape[1]
    input_proj = proj_d[:, : 2 * R]
    output_proj = proj_d[:, 2 * R :]
    block_rows = lax.all_gather(tokens, "hid", axis=0, tiled=True)
    forward = jnp.concatenate(
        [
            project_rows(block_rows, gate_weight),
            project_rows(block_rows, up_weight),
            project_rows(block_rows, input_proj),
        ],
        axis=1,
    )
    block_rows = lax.all_gather(out_grad, "hid", axis=0, tiled=True)
    spread = lax.dot_general(
        block_rows, down_weight, (((1,), (1,)), ((), ())), preferred_element_type=jnp.float32
    )
    backward = jnp.concatenate([spread, project_rows(block_rows, output_proj)], axis=1)
    forward = lax.psum(forward, "mod")
    backward = lax.psum(backward, "mod")
    gate_act = forward[:, :width]
    up_act = forward[:, width : 2 * width]
    input_gate = forward[:, 2 * width : 2 * width + R]
    input_up = forward[:, 2 * width + R :]
    hidden_grad = backward[:, :width]
    output_down = backward[:, width:]
    hidden, gate_grad, up_grad = pointwise(gate_act, up_act, hidden_grad)
    output_gate = project_rows(gate_grad, proj_ff[:, :R])
    output_up = project_rows(up_grad, proj_ff[:, R : 2 * R])
    input_down = project_rows(hidden, proj_ff[:, 2 * R :])
    shares = R // lax.axis_size("hid")
    offset = lax.axis_index("hid") * shares
    output_gate, output_up, input_down = lax.psum((output_gate, output_up, input_down), "hid")
    own_gate = lax.dynamic_slice_in_dim(output_gate, offset, shares, 1)
    own_up = lax.dynamic_slice_in_dim(output_up, offset, shares, 1)
    own_down = lax.dynamic_slice_in_dim(output_down, offset, shares, 1)
    outputs = jnp.stack([own_gate, own_up, own_down], axis=2)
    inputs = jnp.stack([input_gate, input_up, input_down], axis=1)
    total_rows = outputs.shape[0]
    outer = (outputs[:, :, :, None] * inputs[:, None, :, :]).reshape(total_rows, shares * 3 * R)
    examples = example_ids.shape[0] // EX_TOK
    member = (example_ids[None, :] == jnp.arange(examples, dtype=jnp.int32)[:, None]).astype(
        jnp.float32
    )
    features = jnp.dot(member, outer, precision=HIGH, preferred_element_type=jnp.float32)
    partial_scores = jnp.dot(
        features,
        test_features.astype(jnp.float32).T,
        precision=HIGH,
        preferred_element_type=jnp.float32,
    )
    scores = lax.psum(partial_scores, "hid")
    return (features, scores)


def pointwise(gate_act, up_act, hidden_grad):
    sig = jax.nn.sigmoid(gate_act)
    hidden = (gate_act * sig * up_act).astype(jnp.bfloat16)
    gate_grad = (hidden_grad * up_act * sig * (1.0 + gate_act * (1.0 - sig))).astype(jnp.bfloat16)
    up_grad = (hidden_grad * gate_act * sig).astype(jnp.bfloat16)
    return hidden, gate_grad, up_grad


def ring_device(position, core, chips):
    height = chips // 2
    if isinstance(position, int):
        back = position >= height
        z = 2 * height - 1 - position if back else position
        return z * 4 + int(back) * 2 + core
    back = (position >= height).astype(jnp.int32)
    z = position + back * (2 * height - 1 - 2 * position)
    return z * 4 + back * 2 + core


def ring_position(device, chips):
    z, x = device // 4, (device // 2) % 2
    return z + x * (chips - 1 - 2 * z)


def ring_step(block, chips, step):
    pairs = [
        (ring_device(r, core, chips), ring_device((r + step) % chips, core, chips))
        for r in range(chips)
        for core in range(2)
    ]
    return lax.ppermute(block, "hid", pairs)


def core_swap(block, chips):
    return lax.ppermute(block, "hid", [(h, h ^ 1) for h in range(2 * chips)])


def gather_blocks(own, chips, last):
    offsets, blocks = [0], [own]
    ahead, behind = own, own
    for step in range(1, chips // 2):
        ahead = ring_step(ahead, chips, 1)
        behind = ring_step(behind, chips, -1)
        offsets += [-step, step]
        blocks += [ahead, behind]
    offsets.append(chips // 2)
    blocks.append(ring_step(ahead if last > 0 else behind, chips, last))
    return [(offset, other, 0) for other in range(2) for offset in offsets], blocks


def after(value, other):
    return lax.optimization_barrier((value, other))[0]


def assemble(places, chips, blocks, whole, sems):
    device = lax.axis_index("hid")
    position, core = ring_position(device, chips), device % 2
    copies = []
    for index, (offset, other, column) in enumerate(places):
        rows, columns = blocks[index].shape
        source_core = core + other - 2 * core * other
        source = ring_device((position + offset + chips) % chips, source_core, chips)
        start = pl.multiple_of(source * rows, rows)
        target = whole.at[pl.ds(start, rows), pl.ds(column, columns)]
        copies.append(pltpu.make_async_copy(blocks[index], target, sems.at[index]))
    for copy in copies:
        copy.start()
    for copy in copies:
        copy.wait()


def last_dot(a, b):
    return lax.dot_general(a, b, (((1,), (1,)), ((), ())), preferred_element_type=jnp.float32)


def forward_kernel(places, chips, *refs):
    count = len(places)
    blocks, refs = refs[:count], refs[count:]
    gate_weight, up_weight, proj, gate, up, inputs, gate_sum, up_sum, whole, sems = refs
    n, k = pl.program_id(0), pl.program_id(1)

    @pl.when((n == 0) & (k == 0))
    def _():
        assemble(places, chips, blocks, whole, sems)
        inputs[...] = jnp.zeros_like(inputs)

    depth = gate_weight.shape[0]
    x = whole[:, pl.ds(pl.multiple_of(k * depth, depth), depth)]
    gate_part = jnp.dot(x, gate_weight[...], preferred_element_type=jnp.float32)
    up_part = jnp.dot(x, up_weight[...], preferred_element_type=jnp.float32)

    @pl.when(n < PIECES)
    def _():
        piece = depth // PIECES
        part = pl.ds(pl.multiple_of(k * depth + n * piece, piece), piece)
        inputs[...] += last_dot(proj[: 2 * R, part], whole[:, part])

    @pl.when(k == 0)
    def _():
        gate_sum[...] = gate_part
        up_sum[...] = up_part

    @pl.when(k == 1)
    def _():
        gate[...] = (gate_sum[...] + gate_part).T
        up[...] = (up_sum[...] + up_part).T


def forward(places, chips, blocks, gate_weight, up_weight, proj, tile):
    depth, width = gate_weight.shape
    rows = blocks[0].shape[0] * chips * 2
    return pl.pallas_call(
        functools.partial(forward_kernel, places, chips),
        grid=(width // tile, 2),
        out_shape=[jax.ShapeDtypeStruct((width, rows), jnp.float32)] * 2
        + [jax.ShapeDtypeStruct((2 * R, rows), jnp.float32)],
        in_specs=[pl.BlockSpec(memory_space=pl.ANY)] * len(blocks)
        + [pl.BlockSpec((depth // 2, tile), lambda n, k: (k, n))] * 2
        + [pl.BlockSpec((3 * R, depth), lambda n, k: (0, 0))],
        out_specs=[pl.BlockSpec((tile, rows), lambda n, k: (n, 0))] * 2
        + [pl.BlockSpec((2 * R, rows), lambda n, k: (0, 0))],
        scratch_shapes=[
            pltpu.VMEM((rows, tile), jnp.float32),
            pltpu.VMEM((rows, tile), jnp.float32),
            pltpu.VMEM((rows, depth), jnp.bfloat16),
            pltpu.SemaphoreType.DMA((len(blocks),)),
        ],
        compiler_params=pltpu.CompilerParams(vmem_limit_bytes=28 * MEBI),
        cost_estimate=pl.CostEstimate(
            flops=4 * rows * depth * width, bytes_accessed=4 * depth * width, transcendentals=0
        ),
    )(*blocks, gate_weight, up_weight, proj)


def membership(ids, examples):
    rows = lax.broadcasted_iota(jnp.int32, (examples, ids.shape[1]), 0)
    return (jnp.broadcast_to(ids, rows.shape) == rows).astype(jnp.float32)


def exact_dot(a, b, contract):
    return lax.dot_general(
        a, b, (contract, ((), ())), precision=HIGH, preferred_element_type=jnp.float32
    )


def backward_kernel(places, chips, examples, tile, parts, *refs):
    count = len(places)
    blocks, refs = refs[:count], refs[count:]
    weights, refs = refs[:SPLIT], refs[SPLIT:]
    proj, proj_ff, ids = refs[:3]
    gates, ups = refs[3 : 3 + parts], refs[3 + parts : 3 + 2 * parts]
    ready, whole, spread, flipped, sums, sems = refs[3 + 2 * parts :]
    step = pl.program_id(0)
    hid = 2 * chips
    shares = R // hid

    @pl.when(step == 0)
    def _():
        assemble(places, chips, blocks, whole, sems)
        spread[...] = jnp.zeros_like(spread)
        flipped[...] = jnp.zeros_like(flipped)

    height, depth = weights[0].shape
    x = whole[:, pl.ds(pl.multiple_of(step * depth, depth), depth)]
    for q, weight in enumerate(weights):
        spread[q * height : (q + 1) * height, :] += last_dot(weight[...], x)
    turned = last_dot(proj[2 * R :, :], x)
    for lanes in range(flipped.shape[0]):
        flipped[lanes] += turned[:, lanes * 128 : (lanes + 1) * 128]

    @pl.when(step == pl.num_programs(0) - 1)
    def _():
        sums[...] = jnp.zeros_like(sums)
        start = 0
        for gate, up in zip(gates, ups):
            for local in range(0, gate.shape[0], tile):
                part = pl.ds(local, tile)
                hidden, gate_grad, up_grad = pointwise(
                    gate[part, :], up[part, :], spread[start : start + tile, :]
                )
                for m, value in enumerate((gate_grad, up_grad, hidden)):
                    sums[m * R : (m + 1) * R, :] += jnp.dot(
                        proj_ff[m * R : (m + 1) * R, start : start + tile],
                        value,
                        preferred_element_type=jnp.float32,
                    )
                start += tile
        for m in range(2):
            for p in range(hid):
                own = sums[m * R + p * shares : m * R + (p + 1) * shares, :]
                ready[p, m * shares : (m + 1) * shares, :] = own
        member = membership(ids[...], examples)
        total_rows = member.shape[1]
        for j in range(shares):
            every = pl.ds(j, hid, shares)
            own = jnp.concatenate([flipped[k, every, :] for k in range(flipped.shape[0])], axis=1)
            left = (own[:, None, :] * member[None, :, :]).reshape(hid * examples, total_rows)
            product = exact_dot(left, sums[2 * R :, :], ((1,), (1,)))
            ready[:, 2 * shares :, j * R : (j + 1) * R] = product.reshape(hid, examples, R)


def backward(places, chips, blocks, weight, gates, ups, proj, proj_ff, ids, depth_tile, tile):
    rows = blocks[0].shape[0] * chips * 2
    width, depth = weight.shape
    hid = 2 * chips
    shares, examples = R // hid, rows // EX_TOK
    deep = 2 * shares + examples

    def stay(*shape):
        return pl.BlockSpec(shape, lambda k: (0,) * len(shape))

    return pl.pallas_call(
        functools.partial(backward_kernel, places, chips, examples, tile, len(gates)),
        grid=(depth // depth_tile,),
        out_shape=jax.ShapeDtypeStruct((hid, deep, rows), jnp.float32),
        in_specs=[pl.BlockSpec(memory_space=pl.ANY)] * len(blocks)
        + [
            pl.BlockSpec((width // SPLIT, depth_tile), lambda k, q=q: (q, k))
            for q in range(SPLIT)
        ]
        + [
            pl.BlockSpec((3 * R, depth_tile), lambda k: (0, k)),
            stay(3 * R, width),
            stay(1, rows),
        ]
        + [stay(*value.shape) for value in (*gates, *ups)],
        out_specs=stay(hid, deep, rows),
        scratch_shapes=[
            pltpu.VMEM((rows, depth), jnp.bfloat16),
            pltpu.VMEM((width, rows), jnp.float32),
            pltpu.VMEM((rows // 128, R, 128), jnp.float32),
            pltpu.VMEM((3 * R, rows), jnp.float32),
            pltpu.SemaphoreType.DMA((len(blocks),)),
        ],
        compiler_params=pltpu.CompilerParams(vmem_limit_bytes=44 * MEBI),
        cost_estimate=pl.CostEstimate(
            flops=2 * rows * depth * width, bytes_accessed=2 * depth * width, transcendentals=0
        ),
    )(*blocks, *[weight] * SPLIT, proj, proj_ff, ids, *gates, *ups)


def features_kernel(hid, received, inputs, ids, tests, features, partial):
    shares = R // hid
    examples = features.shape[0]
    member = membership(ids[...], examples)
    total = jnp.sum(received[...], axis=0)
    for m in range(2):
        own = total[m * shares : (m + 1) * shares]
        left = (own[:, None, :] * member[None, :, :]).reshape(shares * examples, own.shape[1])
        product = exact_dot(left, inputs[m * R : (m + 1) * R, :], ((1,), (1,)))
        for j in range(shares):
            start = (j * 3 + m) * R
            features[:, start : start + R] = product[j * examples : (j + 1) * examples]
    for j in range(shares):
        start = (j * 3 + 2) * R
        features[:, start : start + R] = total[2 * shares :, j * R : (j + 1) * R]
    scores = exact_dot(features[...], tests[...].astype(jnp.float32), ((1,), (1,)))
    partial[...] = jnp.broadcast_to(scores[None], partial.shape)


def finish(received, inputs, ids, tests):
    hid = received.shape[0]
    examples = ids.shape[1] // EX_TOK
    vmem = pl.BlockSpec(memory_space=pltpu.VMEM)
    return pl.pallas_call(
        functools.partial(features_kernel, hid),
        out_shape=(
            jax.ShapeDtypeStruct((examples, tests.shape[1]), jnp.float32),
            jax.ShapeDtypeStruct((hid, examples, tests.shape[0]), jnp.float32),
        ),
        in_specs=[vmem] * 4,
        out_specs=(vmem, vmem),
        compiler_params=pltpu.CompilerParams(vmem_limit_bytes=24 * MEBI),
    )(received, inputs, ids, tests)


def local_ring(
    tokens,
    out_grad,
    gate_weight,
    up_weight,
    down_weight,
    proj_d,
    proj_ff,
    example_ids,
    test_features,
):
    chips = lax.axis_size("hid") // 2
    ids = example_ids[None, :]
    places, token_blocks = gather_blocks(tokens, chips, 1)
    _, grad_blocks = gather_blocks(out_grad, chips, -1)
    token_blocks = token_blocks + [core_swap(block, chips) for block in token_blocks]
    token_blocks[0] = after(token_blocks[0], grad_blocks[-2])
    gate, up, inputs = forward(
        places, chips, token_blocks, gate_weight, up_weight, proj_d.T, TILE
    )
    early = [core_swap(block, chips) for block in grad_blocks[:-3]]
    late = [core_swap(after(block, gate), chips) for block in grad_blocks[-3:]]
    grad_blocks = grad_blocks + early + late
    send = backward(
        places, chips, grad_blocks, down_weight, [gate], [up], proj_d.T, proj_ff.T, ids, 2048, TILE
    )
    received = lax.all_to_all(send, "hid", 0, 0)
    features, partial = finish(received, inputs, ids, test_features)
    scores = jnp.sum(lax.all_to_all(partial, "hid", 0, 0), axis=0)
    return features, scores


def solution(mesh):
    one_ring = mesh.shape["mod"] == 1 and mesh.shape["hid"] <= 16
    return jax.shard_map(
        local_ring if one_ring else local_general,
        mesh=mesh,
        in_specs=(
            P(("groups", "hid"), "mod"),
            P(("groups", "hid"), "mod"),
            P("mod", "hid"),
            P("mod", "hid"),
            P("hid", "mod"),
            P("mod", None),
            P("hid", None),
            P("groups"),
            P("groups", "hid"),
        ),
        out_specs=(P("groups", "hid"), P("groups", None)),
        check_vma=False,
    )
```
